32 devices in a mesh: dp: 8 (over z, y), owner: 4 (over x, core).
Axes of the slice: x: 2, y: 2, z: 4, core: 2. Of those that a mesh axis runs over, the one named last changes fastest.
Arguments:
- embeddings: bfloat16 [4096, 1024], P(('dp', 'owner')), may hold values from -120 to 120
- assignment: int32 [4096], P(('dp', 'owner')), may hold values from 0 to 511, as said below
- pair_list: int32 [512], replicated, may hold values from 0 to 511, as said below
Outputs:
- best_similarity: float32 [4096], P(('dp', 'owner'))
The draws below stay inside these ranges and needn't reach their ends.
Inputs may be any that keep to these rules, and one draw needn't show every extreme that they name: `assignment`: row r's cluster id is (t * n + o) * 16 + c, where n is the number of owner indices, o the owner index of the device holding row r, t an index of dp and c below 16. Among the rows of one device at most 32 share one t, and on every device exactly 32 rows share some t. pair_list[pair_list[k]] = k for every cluster k; cluster k = (t * n + o) * 16 + c and its partner have the same t and different owner indices o.
All inputs are finite; a program needn't handle non-finite values.
Results may differ from the reference program's by a relative error of at most 0.00053.
Values may be sent and summed in bfloat16 or wider, within the bound.
A program may use at most 64 MiB of HBM per device.

```python
import jax
import jax.numpy as jnp
from jax import lax

D = 1024
ROW_DEV = 128
CPD = 16
CAP = 32
SLOTS = 256
ROWS = 4096
NCL = 512
N_DP = 8
N_OWNER = 4


def layout_draw(key):
    pair_key = jax.random.fold_in(key, 11)
    perm_key, xor_key = jax.random.split(pair_key)
    perms = jax.vmap(lambda k: jax.random.permutation(k, CPD))(jax.random.split(perm_key, N_DP * N_OWNER))
    perms = perms.reshape(N_DP, N_OWNER, CPD).astype(jnp.int32)
    xors = jax.random.randint(xor_key, (N_DP, CPD), 1, N_OWNER).astype(jnp.int32)
    owners = jnp.arange(N_OWNER, dtype=jnp.int32)
    dps = jnp.arange(N_DP, dtype=jnp.int32)
    peer = jnp.bitwise_xor(owners[None, :, None], xors[:, None, :])
    peer_local = jnp.take_along_axis(perms, peer, axis=1)
    partner_id = (dps[:, None, None] * N_OWNER + peer) * CPD + peer_local
    own_id = (dps[:, None, None] * N_OWNER + owners[None, :, None]) * CPD + perms
    pairs = jnp.zeros((NCL,), jnp.int32).at[own_id.reshape(-1)].set(partner_id.reshape(-1))
    row_key = jax.random.fold_in(key, 12)
    spike_key, pick_key, order_key, local_key = jax.random.split(row_key, 4)
    devices = N_DP * N_OWNER
    spike = jax.random.randint(spike_key, (devices,), 0, N_DP).astype(jnp.int32)
    picks = jax.vmap(lambda k: jax.random.permutation(k, (N_DP - 1) * CAP))(jax.random.split(pick_key, devices))
    picks = picks[:, :ROW_DEV - CAP].astype(jnp.int32)
    heads = jnp.broadcast_to(spike[:, None], (devices, CAP))
    others = (spike[:, None] + 1 + picks // CAP) % N_DP
    dest_list = jnp.concatenate([heads, others], axis=1)
    order = jax.vmap(lambda k: jax.random.permutation(k, ROW_DEV))(jax.random.split(order_key, devices)).astype(jnp.int32)
    dest = jnp.take_along_axis(dest_list, order, axis=1)
    local = jax.random.randint(local_key, (devices, ROW_DEV), 0, CPD).astype(jnp.int32)
    owner_of = (jnp.arange(devices, dtype=jnp.int32) % N_OWNER)[:, None]
    assign = ((dest * N_OWNER + owner_of) * CPD + local).reshape(-1)
    return (assign, pairs)


def draw_assignment(key, part):
    assign, pairs = layout_draw(key)
    return assign


def draw_pair_list(key, part):
    assign, pairs = layout_draw(key)
    return pairs


def draw_embeddings(key, part):
    assign, pairs = layout_draw(key)
    emb_key = jax.random.fold_in(key, 13)
    base_key, own_key, amp_key, noise_key = jax.random.split(emb_key, 4)
    base = jax.random.truncated_normal(base_key, -4.0, 4.0, (NCL, D), jnp.float32)
    own = jax.random.truncated_normal(own_key, -4.0, 4.0, (NCL, D), jnp.float32)
    anchor = jnp.minimum(assign, jnp.take(pairs, assign))
    amp = jax.random.uniform(amp_key, (ROWS, 1), jnp.float32, 0.2, 1.4)
    noise = jax.random.truncated_normal(noise_key, -4.0, 4.0, (ROWS, D), jnp.float32)
    values = amp * (0.9 * jnp.take(base, anchor, axis=0) + 0.436 * jnp.take(own, assign, axis=0)) + noise
    return values.astype(jnp.bfloat16)


def setup_inputs(seed: int = 0) -> dict:
    key_of = jax.random.split(jax.random.key(seed), 4)
    return {
        "embeddings": draw_embeddings(jax.random.fold_in(key_of[3], 71), 0),
        "assignment": draw_assignment(jax.random.fold_in(key_of[3], 71), 0),
        "pair_list": draw_pair_list(jax.random.fold_in(key_of[3], 71), 0),
    }


def reference(embeddings, assignment, pair_list):
    values = embeddings.astype(jnp.float32)
    unit = (values * lax.rsqrt(lax.optimization_barrier(jnp.sum(values * values, axis=1, keepdims=True)) + 1e-06)).astype(jnp.bfloat16)
    devices = N_DP * N_OWNER
    target = assignment // (N_OWNER * CPD)
    by_device = target.reshape(devices, ROW_DEV)
    onehot = (by_device[:, :, None] == jnp.arange(N_DP, dtype=jnp.int32)[None, None, :]).astype(jnp.int32)
    slot = (lax.optimization_barrier(jnp.sum(jnp.cumsum(onehot, axis=1) * onehot, axis=2)) - 1).reshape(-1)
    source = jnp.arange(ROWS, dtype=jnp.int32) // ROW_DEV
    source_dp = source // N_OWNER
    source_owner = source % N_OWNER
    flat = (((target * N_OWNER + source_owner) * N_DP + source_dp) * CAP + slot).astype(jnp.int32)
    table = jnp.zeros((N_DP * N_OWNER * SLOTS, D), jnp.bfloat16).at[flat].set(unit)
    table = table.reshape(N_DP, N_OWNER, SLOTS, D)
    table_ids = jnp.full((N_DP * N_OWNER * SLOTS,), -1, jnp.int32).at[flat].set(assignment)
    table_ids = table_ids.reshape(N_DP, N_OWNER, SLOTS)

    def group(item):
        rows_t, ids_t = item
        every_row = rows_t.reshape(N_OWNER * SLOTS, D)
        every_id = ids_t.reshape(N_OWNER * SLOTS)
        column = jnp.arange(N_OWNER * SLOTS, dtype=jnp.int32)

        def one_owner(owner_index):
            mine = rows_t[owner_index]
            mine_ids = ids_t[owner_index]
            partner = jnp.take(pair_list, jnp.maximum(mine_ids, 0))
            scores = jnp.dot(mine.astype(jnp.float32), every_row.astype(jnp.float32).T)
            itself = owner_index * SLOTS + jnp.arange(SLOTS, dtype=jnp.int32)
            same = (mine_ids[:, None] == every_id[None, :]) & (every_id[None, :] >= 0) & (itself[:, None] != column[None, :])
            related = same | (partner[:, None] == every_id[None, :])
            return jnp.maximum(-1.0, lax.optimization_barrier(jnp.max(jnp.where(related, scores, -1.0), axis=1)))
        return lax.map(one_owner, jnp.arange(N_OWNER, dtype=jnp.int32))
    best = lax.map(group, (table, table_ids))
    return best.reshape(-1)[flat]
```

```python
import functools

import jax
import jax.numpy as jnp
from jax import lax
from jax.experimental import pallas as pl
from jax.experimental.pallas import tpu as pltpu
from jax.sharding import PartitionSpec as P

CPD = 16
MESH = pl.DeviceIdType.MESH
NT = (((1,), (1,)), ((), ()))


def peer_of(d, k):
    z, y = d // 2, d % 2
    dz, dy = k // 2, k % 2
    if dz == 1:
        z = z + 1 - 2 * (z % 2)
    elif dz == 2:
        z = (z + 2) % 4
    elif dz == 3:
        z = 3 - z
    if dy:
        y = 1 - y
    return z * 2 + y


SEND_ORDER = (4, 5, 6, 7, 2, 3, 1)
WAIT_ORDER = (1, 2, 3, 4, 6, 5, 7)


def kernel(
    cap, n_dp, n_owner,
    emb, asg, pairs, out,
    send, own, sib, cpt,
    code_send, code_got, codes, ret, res,
    row_ss, row_rs, id_ss, id_rs, fw_ss, fw_rs, cd_ss, cd_rs, rt_ss, rt_rs,
):
    rows, width = emb.shape
    slots = cap * n_dp
    d = lax.axis_index("dp")
    o = lax.axis_index("owner")
    o_sib = o + 1 - 2 * (o % 2)
    o_cpt = (o + 2) % 4
    peers = [peer_of(d, k) for k in range(n_dp)]

    barrier = pltpu.get_barrier_semaphore()
    for k in range(n_dp):
        if k:
            pl.semaphore_signal(barrier, inc=1, device_id=(peers[k], o), device_id_type=MESH)
        pl.semaphore_signal(barrier, inc=1, device_id=(peers[k], o_sib), device_id_type=MESH)
    pl.semaphore_signal(barrier, inc=1, device_id=(d, o_cpt), device_id_type=MESH)

    a = asg[...]
    t_row = lax.shift_right_logical(a, 6)
    code_row = ((a & 63) + 1).astype(jnp.float32)
    t_hot = (lax.broadcasted_iota(jnp.int32, (n_dp, rows), 0) == t_row).astype(jnp.float32)
    before = (
        lax.broadcasted_iota(jnp.int32, (rows, rows), 0)
        < lax.broadcasted_iota(jnp.int32, (rows, rows), 1)
    ).astype(jnp.float32).astype(jnp.bfloat16)
    count = jnp.dot(t_hot.astype(jnp.bfloat16), before, preferred_element_type=jnp.float32)
    rank = jnp.sum(t_hot * count, axis=0, keepdims=True).astype(jnp.int32)
    slot_iota = lax.broadcasted_iota(jnp.int32, (slots, rows), 0)
    lane_hot = (slot_iota == d * cap + rank).astype(jnp.float32)
    slot_codes = lax.dot_general(
        (t_hot * code_row).astype(jnp.bfloat16),
        lane_hot.astype(jnp.bfloat16),
        NT,
        preferred_element_type=jnp.float32,
    )
    for t in range(n_dp):
        code_send[t] = slot_codes[t : t + 1, :]

    values = emb[...].astype(jnp.float32)
    unit = (values * lax.rsqrt(jnp.sum(values * values, axis=1, keepdims=True) + 1e-06)).astype(
        jnp.bfloat16
    )
    place = (slot_iota == t_row * cap + rank).astype(jnp.float32).astype(jnp.bfloat16)
    packed = jnp.dot(place, unit, preferred_element_type=jnp.float32).astype(jnp.bfloat16)
    for t in range(n_dp):
        send[t] = packed[t * cap : (t + 1) * cap, :]
    own[d] = send[d]
    code_got[d] = code_send[d]

    pl.semaphore_wait(barrier, 2 * n_dp)

    def block_copy(k):
        p = peers[k]
        return pltpu.make_async_remote_copy(
            src_ref=send.at[p], dst_ref=own.at[d], send_sem=row_ss.at[k], recv_sem=row_rs.at[k],
            device_id=(p, o), device_id_type=MESH,
        )

    def code_copy(k):
        p = peers[k]
        return pltpu.make_async_remote_copy(
            src_ref=code_send.at[p], dst_ref=code_got.at[d], send_sem=id_ss.at[k],
            recv_sem=id_rs.at[k], device_id=(p, o), device_id_type=MESH,
        )

    def forward(k, which):
        s = peers[k]
        return pltpu.make_async_remote_copy(
            src_ref=own.at[s], dst_ref=(sib, cpt)[which].at[s], send_sem=fw_ss.at[which, k],
            recv_sem=fw_rs.at[which, k], device_id=(d, (o_sib, o_cpt)[which]), device_id_type=MESH,
        )

    def codes_copy(which):
        return pltpu.make_async_remote_copy(
            src_ref=codes.at[0], dst_ref=codes.at[1 + which], send_sem=cd_ss.at[which],
            recv_sem=cd_rs.at[which], device_id=(d, (o_sib, o_cpt)[which]), device_id_type=MESH,
        )

    def back(k, which):
        s = peers[k]
        return pltpu.make_async_remote_copy(
            src_ref=res.at[which], dst_ref=ret.at[which, d], send_sem=rt_ss.at[which, k],
            recv_sem=rt_rs.at[which, k], device_id=(s, (o, o_sib)[which]), device_id_type=MESH,
        )

    for k in SEND_ORDER:
        code_copy(k).start()
    for k in SEND_ORDER:
        block_copy(k).start()
    forward(0, 1).start()
    forward(0, 0).start()
    for k in WAIT_ORDER:
        code_copy(k).wait_recv()
    codes[0] = jnp.sum(code_got[...], axis=0)
    codes_copy(0).start()
    codes_copy(1).start()
    for k in WAIT_ORDER:
        block_copy(k).wait_recv()
        forward(k, 1).start()
        forward(k, 0).start()

    codes_copy(0).wait_recv()
    codes_copy(1).wait_recv()
    g_own, g_sib, g_cpt = codes[0], codes[1], codes[2]

    def partner(g, owner):
        found = jnp.full(g.shape, -1, jnp.int32)
        for c in range(CPD):
            other = pairs[(d * n_owner + owner) * CPD + c] - d * (n_owner * CPD) + 1
            found = jnp.where(g == (owner * CPD + c + 1).astype(jnp.float32), other, found)
        return found.astype(jnp.float32)

    p_own, p_sib = partner(g_own, o), partner(g_sib, o_sib)

    def column(g):
        return jnp.transpose(jnp.broadcast_to(g, (128, slots)))

    def table(ref):
        return ref[...].reshape(slots, width)

    def scores(keys, queries):
        return lax.dot_general(keys, queries, NT, preferred_element_type=jnp.float32)

    def wide(column_128):
        return jnp.concatenate([column_128] * (slots // 128), axis=1)

    def masked_max(s, mask):
        return jnp.max(jnp.where(mask, s, -1.0), axis=0, keepdims=True)

    rows_own = table(own)
    key = lax.broadcasted_iota(jnp.int32, (slots, slots), 0)
    query = lax.broadcasted_iota(jnp.int32, (slots, slots), 1)
    best = masked_max(scores(rows_own, rows_own), (wide(column(g_own)) == g_own) & (key != query))
    for k in range(n_dp):
        forward(k, 0).wait_recv()
    rows_sib = table(sib)
    best = jnp.maximum(best, masked_max(scores(rows_sib, rows_own), wide(column(g_sib)) == p_own))
    for k in range(n_dp):
        forward(k, 1).wait_recv()
    rows_cpt = table(cpt)
    k_cpt = wide(column(g_cpt))
    res[1] = masked_max(scores(rows_cpt, rows_sib), k_cpt == p_sib)
    for k in (4, 5, 6, 7, 2, 3, 1, 0):
        back(k, 1).start()
    best = jnp.maximum(best, masked_max(scores(rows_cpt, rows_own), k_cpt == p_own))
    res[0] = best
    for k in SEND_ORDER:
        back(k, 0).start()
    ret[0, d] = best

    for k in range(n_dp):
        back(k, 1).wait_recv()
        if k:
            back(k, 0).wait_recv()
    got = jnp.concatenate([jnp.maximum(ret[0, t], ret[1, t]) for t in range(n_dp)], axis=0)
    picked = lax.dot_general(
        got, lane_hot, (((1,), (0,)), ((), ())),
        preferred_element_type=jnp.float32, precision=lax.Precision.HIGHEST,
    )
    out[...] = jnp.maximum(jnp.sum(t_hot * picked, axis=0, keepdims=True), -1.0)

    for k in range(n_dp):
        if k:
            block_copy(k).wait_send()
            code_copy(k).wait_send()
            back(k, 0).wait_send()
        back(k, 1).wait_send()
        forward(k, 0).wait_send()
        forward(k, 1).wait_send()
    codes_copy(0).wait_send()
    codes_copy(1).wait_send()


def fused(embeddings, assignment, pair_list, capacity, n_dp, n_owner):
    rows, width = embeddings.shape
    slots = capacity * n_dp
    block = pltpu.VMEM((n_dp, capacity, width), jnp.bfloat16)
    line = pltpu.VMEM((n_dp, 1, slots), jnp.float32)
    dma = pltpu.SemaphoreType.DMA
    best = pl.pallas_call(
        functools.partial(kernel, capacity, n_dp, n_owner),
        out_shape=jax.ShapeDtypeStruct((1, rows), jnp.float32),
        in_specs=[
            pl.BlockSpec(memory_space=pltpu.VMEM),
            pl.BlockSpec(memory_space=pltpu.VMEM),
            pl.BlockSpec(memory_space=pltpu.SMEM),
        ],
        out_specs=pl.BlockSpec(memory_space=pltpu.VMEM),
        scratch_shapes=[
            block, block, block, block,
            line, line,
            pltpu.VMEM((3, 1, slots), jnp.float32),
            pltpu.VMEM((2, n_dp, 1, slots), jnp.float32),
            pltpu.VMEM((2, 1, slots), jnp.float32),
            dma((n_dp,)), dma((n_dp,)), dma((n_dp,)), dma((n_dp,)),
            dma((2, n_dp)), dma((2, n_dp)), dma((2,)), dma((2,)),
            dma((2, n_dp)), dma((2, n_dp)),
        ],
        compiler_params=pltpu.CompilerParams(
            collective_id=0, has_side_effects=True, vmem_limit_bytes=32 * 1024 * 1024
        ),
    )(embeddings, assignment.reshape(1, rows), pair_list)
    return best.reshape(rows)


def general(embeddings, assignment, pair_list, capacity, n_dp, n_owner):
    rows, width = embeddings.shape
    slots = capacity * n_dp
    values = embeddings.astype(jnp.float32)
    unit = (values * lax.rsqrt(jnp.sum(values * values, axis=1, keepdims=True) + 1e-06)).astype(
        jnp.bfloat16
    )
    target = assignment // (n_owner * CPD)
    onehot = (target[:, None] == jnp.arange(n_dp, dtype=jnp.int32)[None, :]).astype(jnp.int32)
    slot = jnp.sum(jnp.cumsum(onehot, axis=0) * onehot, axis=1) - 1
    position = target * capacity + slot
    here_owner = lax.axis_index("owner")
    here_dp = lax.axis_index("dp")
    first_id = (here_dp * n_owner + here_owner) * CPD
    partners_mine = lax.dynamic_slice_in_dim(pair_list, first_id, CPD)
    start_best = jnp.full((slots,), -1.0, jnp.float32)
    send_rows = jnp.zeros((slots, width), jnp.bfloat16).at[position].set(unit)
    send_ids = jnp.full((slots,), -1, jnp.int32).at[position].set(assignment)
    got_rows, got_ids = (
        lax.all_to_all(
            send_rows.reshape(n_dp, capacity, width), "dp", split_axis=0, concat_axis=0, tiled=True
        ),
        lax.all_to_all(
            send_ids.reshape(n_dp, capacity), "dp", split_axis=0, concat_axis=0, tiled=True
        ),
    )
    mine = got_rows.reshape(slots, width)
    mine_ids = got_ids.reshape(slots)
    local = jnp.clip(mine_ids - first_id, 0, CPD - 1)
    picked = local[:, None] == jnp.arange(CPD, dtype=jnp.int32)[None, :]
    partner = jnp.sum(jnp.where(picked, partners_mine[None, :], 0), axis=1)
    rows_p = lax.all_gather(mine, "owner", axis=0, tiled=True)
    ids_p = lax.all_gather(mine_ids, "owner", axis=0, tiled=True)
    scores = lax.dot_general(mine, rows_p, NT, preferred_element_type=jnp.float32)
    column = jnp.arange(ids_p.shape[0], dtype=jnp.int32)
    itself = here_owner * slots + jnp.arange(slots, dtype=jnp.int32)
    same = (
        (mine_ids[:, None] == ids_p[None, :])
        & (ids_p[None, :] >= 0)
        & (itself[:, None] != column[None, :])
    )
    related = same | (partner[:, None] == ids_p[None, :])
    best = jnp.maximum(start_best, jnp.max(jnp.where(related, scores, -1.0), axis=1))
    returned = lax.all_to_all(
        best.reshape(n_dp, capacity), "dp", split_axis=0, concat_axis=0, tiled=True
    )
    return returned.reshape(slots)[position]


def shards(embeddings, assignment, pair_list):
    n_dp = lax.axis_size("dp")
    n_owner = lax.axis_size("owner")
    capacity = 2 * embeddings.shape[0] // n_dp
    whole_tiles = n_dp == 8 and n_owner == 4 and capacity % 16 == 0
    form = fused if whole_tiles else general
    return form(embeddings, assignment, pair_list, capacity, n_dp, n_owner)


def solution(mesh):
    placed = (P(("dp", "owner"), None), P(("dp", "owner")), P())
    return jax.shard_map(
        shards, mesh=mesh, in_specs=placed, out_specs=P(("dp", "owner")), check_vma=False
    )
```

```python
import functools

import jax
import jax.numpy as jnp
from jax import lax
from jax.experimental import pallas as pl
from jax.experimental.pallas import tpu as pltpu
from jax.sharding import PartitionSpec as P

CPD = 16
MESH = pl.DeviceIdType.MESH
NT = (((1,), (1,)), ((), ()))


def peer_of(d, k):
    z, y = d // 2, d % 2
    dz, dy = k // 2, k % 2
    if dz == 1:
        z = z + 1 - 2 * (z % 2)
    elif dz == 2:
        z = (z + 2) % 4
    elif dz == 3:
        z = 3 - z
    if dy:
        y = 1 - y
    return z * 2 + y


NEAR = (1, 2, 3)
CROSS = (4, 6, 5, 7)
SEND_ORDER = (4, 6, 5, 7, 2, 3, 1)


def kernel(
    cap, n_dp, n_owner,
    emb_hbm, asg_hbm, pairs_hbm, out,
    emb, asg, pairs,
    send, own, sib, cpt,
    code_send, code_got, codes, columns, ret, res,
    in_s,
    row_ss, row_rs, id_ss, id_rs, fw_ss, fw_rs, cd_ss, cd_rs, rt_ss, rt_rs,
):
    rows, width = emb.shape
    slots = cap * n_dp
    loads = [
        pltpu.make_async_copy(src, dst, in_s.at[i])
        for i, (src, dst) in enumerate(((asg_hbm, asg), (emb_hbm, emb), (pairs_hbm, pairs)))
    ]
    for load in loads:
        load.start()
    d = lax.axis_index("dp")
    o = lax.axis_index("owner")
    o_sib = o + 1 - 2 * (o % 2)
    o_cpt = (o + 2) % 4
    peers = [peer_of(d, k) for k in range(n_dp)]

    barrier = pltpu.get_barrier_semaphore()
    for k in range(n_dp):
        if k:
            pl.semaphore_signal(barrier, inc=1, device_id=(peers[k], o), device_id_type=MESH)
        pl.semaphore_signal(barrier, inc=1, device_id=(peers[k], o_sib), device_id_type=MESH)
    pl.semaphore_signal(barrier, inc=1, device_id=(d, o_cpt), device_id_type=MESH)

    loads[0].wait()
    a = asg[...]
    t_row = lax.shift_right_logical(a, 6)
    code_row = ((a & 63) + 1).astype(jnp.float32)
    t_hot = (lax.broadcasted_iota(jnp.int32, (n_dp, rows), 0) == t_row).astype(jnp.float32)
    before = (
        lax.broadcasted_iota(jnp.int32, (rows, rows), 0)
        < lax.broadcasted_iota(jnp.int32, (rows, rows), 1)
    ).astype(jnp.float32).astype(jnp.bfloat16)
    count = jnp.dot(t_hot.astype(jnp.bfloat16), before, preferred_element_type=jnp.float32)
    rank = jnp.sum(t_hot * count, axis=0, keepdims=True).astype(jnp.int32)
    slot_iota = lax.broadcasted_iota(jnp.int32, (slots, rows), 0)
    lane_hot = (slot_iota == d * cap + rank).astype(jnp.float32)
    slot_codes = lax.dot_general(
        (t_hot * code_row).astype(jnp.bfloat16),
        lane_hot.astype(jnp.bfloat16),
        NT,
        preferred_element_type=jnp.float32,
    )
    for t in range(n_dp):
        code_send[t] = slot_codes[t : t + 1, :]

    loads[1].wait()
    values = emb[...].astype(jnp.float32)
    unit = (values * lax.rsqrt(jnp.sum(values * values, axis=1, keepdims=True) + 1e-06)).astype(
        jnp.bfloat16
    )
    place = (slot_iota == t_row * cap + rank).astype(jnp.float32).astype(jnp.bfloat16)
    packed = jnp.dot(place, unit, preferred_element_type=jnp.float32).astype(jnp.bfloat16)
    for t in range(n_dp):
        send[t] = packed[t * cap : (t + 1) * cap, :]
    own[d] = send[d]
    code_got[d] = code_send[d]

    pl.semaphore_wait(barrier, 2 * n_dp)

    def block_copy(k):
        p = peers[k]
        return pltpu.make_async_remote_copy(
            src_ref=send.at[p], dst_ref=own.at[d], send_sem=row_ss.at[k], recv_sem=row_rs.at[k],
            device_id=(p, o), device_id_type=MESH,
        )

    def code_copy(k):
        p = peers[k]
        return pltpu.make_async_remote_copy(
            src_ref=code_send.at[p], dst_ref=code_got.at[d], send_sem=id_ss.at[k],
            recv_sem=id_rs.at[k], device_id=(p, o), device_id_type=MESH,
        )

    def forward(k, which):
        s = peers[k]
        return pltpu.make_async_remote_copy(
            src_ref=own.at[s], dst_ref=(sib, cpt)[which].at[s], send_sem=fw_ss.at[which, k],
            recv_sem=fw_rs.at[which, k], device_id=(d, (o_sib, o_cpt)[which]), device_id_type=MESH,
        )

    def codes_copy(which):
        return pltpu.make_async_remote_copy(
            src_ref=codes.at[0], dst_ref=codes.at[1 + which], send_sem=cd_ss.at[which],
            recv_sem=cd_rs.at[which], device_id=(d, (o_sib, o_cpt)[which]), device_id_type=MESH,
        )

    def back(k, which):
        s = peers[k]
        return pltpu.make_async_remote_copy(
            src_ref=res.at[which], dst_ref=ret.at[which, d], send_sem=rt_ss.at[which, k],
            recv_sem=rt_rs.at[which, k], device_id=(s, (o, o_sib)[which]), device_id_type=MESH,
        )

    for k in CROSS[:2]:
        block_copy(k).start()
    forward(0, 1).start()
    for k in NEAR:
        block_copy(k).start()
    for k in SEND_ORDER:
        code_copy(k).start()
    forward(0, 0).start()
    for i, k in enumerate(NEAR):
        block_copy(k).wait_recv()
        forward(k, 1).start()
        forward(k, 0).start()
        if i < 2:
            block_copy(CROSS[2 + i]).start()
    for k in NEAR + CROSS:
        code_copy(k).wait_recv()
    codes[0] = jnp.sum(code_got[...], axis=0)
    codes_copy(0).start()
    codes_copy(1).start()
    loads[2].wait()
    g_own = codes[0]

    def partner(g, owner):
        found = jnp.full(g.shape, -1, jnp.int32)
        for c in range(CPD):
            other = pairs[(d * n_owner + owner) * CPD + c] - d * (n_owner * CPD) + 1
            found = jnp.where(g == (owner * CPD + c + 1).astype(jnp.float32), other, found)
        return found.astype(jnp.float32)

    def column(g):
        return jnp.transpose(jnp.broadcast_to(g, (128, slots)))

    p_own = partner(g_own, o)
    columns[0] = column(g_own)
    block_copy(CROSS[0]).wait_recv()
    forward(CROSS[0], 1).start()
    forward(CROSS[0], 0).start()
    codes_copy(0).wait_recv()
    codes_copy(1).wait_recv()
    p_sib = partner(codes[1], o_sib)
    columns[1] = column(codes[1])
    columns[2] = column(codes[2])
    for k in CROSS[1:]:
        block_copy(k).wait_recv()
        forward(k, 1).start()
        forward(k, 0).start()

    def table(ref):
        return ref[...].reshape(slots, width)

    def scores(keys, queries):
        return lax.dot_general(keys, queries, NT, preferred_element_type=jnp.float32)

    def wide(which):
        return jnp.concatenate([columns[which]] * (slots // 128), axis=1)

    def masked_max(s, mask):
        return jnp.max(jnp.where(mask, s, -1.0), axis=0, keepdims=True)

    rows_own = table(own)
    key = lax.broadcasted_iota(jnp.int32, (slots, slots), 0)
    query = lax.broadcasted_iota(jnp.int32, (slots, slots), 1)
    best = masked_max(scores(rows_own, rows_own), (wide(0) == g_own) & (key != query))
    for k in range(n_dp):
        forward(k, 0).wait_recv()
    rows_sib = table(sib)
    best = jnp.maximum(best, masked_max(scores(rows_sib, rows_own), wide(1) == p_own))
    for k in range(n_dp):
        forward(k, 1).wait_recv()
    rows_cpt = table(cpt)
    k_cpt = wide(2)
    res[1] = masked_max(scores(rows_cpt, rows_sib), k_cpt == p_sib)
    for k in (4, 5, 6, 7, 2, 3, 1, 0):
        back(k, 1).start()
    best = jnp.maximum(best, masked_max(scores(rows_cpt, rows_own), k_cpt == p_own))
    res[0] = best
    for k in SEND_ORDER:
        back(k, 0).start()
    ret[0, d] = best

    for k in range(n_dp):
        back(k, 1).wait_recv()
        if k:
            back(k, 0).wait_recv()
    got = jnp.concatenate([jnp.maximum(ret[0, t], ret[1, t]) for t in range(n_dp)], axis=0)
    picked = lax.dot_general(
        got, lane_hot, (((1,), (0,)), ((), ())),
        preferred_element_type=jnp.float32, precision=lax.Precision.HIGHEST,
    )
    out[...] = jnp.sum(t_hot * picked, axis=0, keepdims=True)

    for k in range(n_dp):
        if k:
            block_copy(k).wait_send()
            code_copy(k).wait_send()
            back(k, 0).wait_send()
        back(k, 1).wait_send()
        forward(k, 0).wait_send()
        forward(k, 1).wait_send()
    codes_copy(0).wait_send()
    codes_copy(1).wait_send()


def fused(embeddings, assignment, pair_list, capacity, n_dp, n_owner):
    rows, width = embeddings.shape
    slots = capacity * n_dp
    block = pltpu.VMEM((n_dp, capacity, width), jnp.bfloat16)
    line = pltpu.VMEM((n_dp, 1, slots), jnp.float32)
    dma = pltpu.SemaphoreType.DMA
    best = pl.pallas_call(
        functools.partial(kernel, capacity, n_dp, n_owner),
        out_shape=jax.ShapeDtypeStruct((1, rows), jnp.float32),
        in_specs=[pl.BlockSpec(memory_space=pl.ANY)] * 3,
        out_specs=pl.BlockSpec(memory_space=pltpu.VMEM),
        scratch_shapes=[
            pltpu.VMEM((rows, width), jnp.bfloat16),
            pltpu.VMEM((1, rows), jnp.int32),
            pltpu.SMEM(pair_list.shape, jnp.int32),
            block, block, block, block,
            line, line,
            pltpu.VMEM((3, 1, slots), jnp.float32),
            pltpu.VMEM((3, slots, 128), jnp.float32),
            pltpu.VMEM((2, n_dp, 1, slots), jnp.float32),
            pltpu.VMEM((2, 1, slots), jnp.float32),
            dma((3,)),
            dma((n_dp,)), dma((n_dp,)), dma((n_dp,)), dma((n_dp,)),
            dma((2, n_dp)), dma((2, n_dp)), dma((2,)), dma((2,)),
            dma((2, n_dp)), dma((2, n_dp)),
        ],
        compiler_params=pltpu.CompilerParams(
            collective_id=0, has_side_effects=True, vmem_limit_bytes=60 * 1024 * 1024
        ),
    )(embeddings, assignment.reshape(1, rows), pair_list)
    return jnp.maximum(best.reshape(rows), -1.0)


def general(embeddings, assignment, pair_list, capacity, n_dp, n_owner):
    rows, width = embeddings.shape
    slots = capacity * n_dp
    values = embeddings.astype(jnp.float32)
    unit = (values * lax.rsqrt(jnp.sum(values * values, axis=1, keepdims=True) + 1e-06)).astype(
        jnp.bfloat16
    )
    target = assignment // (n_owner * CPD)
    onehot = (target[:, None] == jnp.arange(n_dp, dtype=jnp.int32)[None, :]).astype(jnp.int32)
    slot = jnp.sum(jnp.cumsum(onehot, axis=0) * onehot, axis=1) - 1
    position = target * capacity + slot
    here_owner = lax.axis_index("owner")
    here_dp = lax.axis_index("dp")
    first_id = (here_dp * n_owner + here_owner) * CPD
    partners_mine = lax.dynamic_slice_in_dim(pair_list, first_id, CPD)
    start_best = jnp.full((slots,), -1.0, jnp.float32)
    send_rows = jnp.zeros((slots, width), jnp.bfloat16).at[position].set(unit)
    send_ids = jnp.full((slots,), -1, jnp.int32).at[position].set(assignment)
    got_rows, got_ids = (
        lax.all_to_all(
            send_rows.reshape(n_dp, capacity, width), "dp", split_axis=0, concat_axis=0, tiled=True
        ),
        lax.all_to_all(
            send_ids.reshape(n_dp, capacity), "dp", split_axis=0, concat_axis=0, tiled=True
        ),
    )
    mine = got_rows.reshape(slots, width)
    mine_ids = got_ids.reshape(slots)
    local = jnp.clip(mine_ids - first_id, 0, CPD - 1)
    picked = local[:, None] == jnp.arange(CPD, dtype=jnp.int32)[None, :]
    partner = jnp.sum(jnp.where(picked, partners_mine[None, :], 0), axis=1)
    rows_p = lax.all_gather(mine, "owner", axis=0, tiled=True)
    ids_p = lax.all_gather(mine_ids, "owner", axis=0, tiled=True)
    scores = lax.dot_general(mine, rows_p, NT, preferred_element_type=jnp.float32)
    column = jnp.arange(ids_p.shape[0], dtype=jnp.int32)
    itself = here_owner * slots + jnp.arange(slots, dtype=jnp.int32)
    same = (
        (mine_ids[:, None] == ids_p[None, :])
        & (ids_p[None, :] >= 0)
        & (itself[:, None] != column[None, :])
    )
    related = same | (partner[:, None] == ids_p[None, :])
    best = jnp.maximum(start_best, jnp.max(jnp.where(related, scores, -1.0), axis=1))
    returned = lax.all_to_all(
        best.reshape(n_dp, capacity), "dp", split_axis=0, concat_axis=0, tiled=True
    )
    return returned.reshape(slots)[position]


def shards(embeddings, assignment, pair_list):
    n_dp = lax.axis_size("dp")
    n_owner = lax.axis_size("owner")
    capacity = 2 * embeddings.shape[0] // n_dp
    whole_tiles = n_dp == 8 and n_owner == 4 and capacity % 16 == 0
    form = fused if whole_tiles else general
    return form(embeddings, assignment, pair_list, capacity, n_dp, n_owner)


def solution(mesh):
    placed = (P(("dp", "owner"), None), P(("dp", "owner")), P())
    return jax.shard_map(
        shards, mesh=mesh, in_specs=placed, out_specs=P(("dp", "owner")), check_vma=False
    )
```

```python
import functools

import jax
import jax.numpy as jnp
from jax import lax
from jax.experimental import pallas as pl
from jax.experimental.pallas import tpu as pltpu
from jax.sharding import PartitionSpec as P

CPD = 16
MESH = pl.DeviceIdType.MESH
NT = (((1,), (1,)), ((), ()))


def peer_of(d, k):
    z, y = d // 2, d % 2
    dz, dy = k // 2, k % 2
    if dz == 1:
        z = z + 1 - 2 * (z % 2)
    elif dz == 2:
        z = (z + 2) % 4
    elif dz == 3:
        z = 3 - z
    if dy:
        y = 1 - y
    return z * 2 + y


NEAR = (1, 2, 3)
CROSS = (4, 6, 5, 7)
PIECES = tuple((k, h) for k in CROSS for h in range(2))
AHEAD = 3
SEND_ORDER = (4, 6, 5, 7, 2, 3, 1)


def kernel(
    cap, n_dp, n_owner,
    emb_hbm, asg_hbm, pairs_hbm, out,
    emb, asg, pairs,
    send, own, sib, cpt,
    code_send, code_got, codes, columns, ret, res,
    in_s,
    row_ss, row_rs, id_ss, id_rs, fw_ss, fw_rs, cd_ss, cd_rs, rt_ss, rt_rs,
):
    rows, width = emb.shape
    slots = cap * n_dp
    loads = [
        pltpu.make_async_copy(src, dst, in_s.at[i])
        for i, (src, dst) in enumerate(((asg_hbm, asg), (emb_hbm, emb), (pairs_hbm, pairs)))
    ]
    for load in loads:
        load.start()
    d = lax.axis_index("dp")
    o = lax.axis_index("owner")
    o_sib = o + 1 - 2 * (o % 2)
    o_cpt = (o + 2) % 4
    peers = [peer_of(d, k) for k in range(n_dp)]

    barrier = pltpu.get_barrier_semaphore()
    for k in range(n_dp):
        if k:
            pl.semaphore_signal(barrier, inc=1, device_id=(peers[k], o), device_id_type=MESH)
        pl.semaphore_signal(barrier, inc=1, device_id=(peers[k], o_sib), device_id_type=MESH)
    pl.semaphore_signal(barrier, inc=1, device_id=(d, o_cpt), device_id_type=MESH)

    loads[0].wait()
    a = asg[...]
    t_row = lax.shift_right_logical(a, 6)
    code_row = ((a & 63) + 1).astype(jnp.float32)
    t_hot = (lax.broadcasted_iota(jnp.int32, (n_dp, rows), 0) == t_row).astype(jnp.float32)
    before = (
        lax.broadcasted_iota(jnp.int32, (rows, rows), 0)
        < lax.broadcasted_iota(jnp.int32, (rows, rows), 1)
    ).astype(jnp.float32).astype(jnp.bfloat16)
    count = jnp.dot(t_hot.astype(jnp.bfloat16), before, preferred_element_type=jnp.float32)
    rank = jnp.sum(t_hot * count, axis=0, keepdims=True).astype(jnp.int32)
    slot_iota = lax.broadcasted_iota(jnp.int32, (slots, rows), 0)
    lane_hot = (slot_iota == d * cap + rank).astype(jnp.float32)
    slot_codes = lax.dot_general(
        (t_hot * code_row).astype(jnp.bfloat16),
        lane_hot.astype(jnp.bfloat16),
        NT,
        preferred_element_type=jnp.float32,
    )
    for t in range(n_dp):
        code_send[t] = slot_codes[t : t + 1, :]

    loads[1].wait()
    values = emb[...].astype(jnp.float32)
    unit = (values * lax.rsqrt(jnp.sum(values * values, axis=1, keepdims=True) + 1e-06)).astype(
        jnp.bfloat16
    )
    position = t_row * cap + rank
    half = n_dp // 2
    near_base = (d // half) * half
    cross_base = half - near_base
    group_iota = lax.broadcasted_iota(jnp.int32, (half * cap, rows), 0)

    def pack(base):
        place = (group_iota + base * cap == position).astype(jnp.float32).astype(jnp.bfloat16)
        packed = jnp.dot(place, unit, preferred_element_type=jnp.float32).astype(jnp.bfloat16)
        send[pl.ds(base, half)] = packed.reshape(half, cap, width)

    pack(cross_base)
    code_got[d] = code_send[d]

    pl.semaphore_wait(barrier, 2 * n_dp)

    def part(h):
        return pl.ds(0, cap) if h is None else pl.ds(h * (cap // 2), cap // 2)

    def block_copy(k, h=None):
        p = peers[k]
        return pltpu.make_async_remote_copy(
            src_ref=send.at[p, part(h)], dst_ref=own.at[d, part(h)],
            send_sem=row_ss.at[k, h or 0], recv_sem=row_rs.at[k, h or 0],
            device_id=(p, o), device_id_type=MESH,
        )

    def code_copy(k):
        p = peers[k]
        return pltpu.make_async_remote_copy(
            src_ref=code_send.at[p], dst_ref=code_got.at[d], send_sem=id_ss.at[k],
            recv_sem=id_rs.at[k], device_id=(p, o), device_id_type=MESH,
        )

    def forward(k, which, h=None):
        s = peers[k]
        return pltpu.make_async_remote_copy(
            src_ref=own.at[s, part(h)], dst_ref=(sib, cpt)[which].at[s, part(h)],
            send_sem=fw_ss.at[which, k, h or 0], recv_sem=fw_rs.at[which, k, h or 0],
            device_id=(d, (o_sib, o_cpt)[which]), device_id_type=MESH,
        )

    def codes_copy(which):
        return pltpu.make_async_remote_copy(
            src_ref=codes.at[0], dst_ref=codes.at[1 + which], send_sem=cd_ss.at[which],
            recv_sem=cd_rs.at[which], device_id=(d, (o_sib, o_cpt)[which]), device_id_type=MESH,
        )

    def back(k, which):
        s = peers[k]
        return pltpu.make_async_remote_copy(
            src_ref=res.at[which], dst_ref=ret.at[which, d], send_sem=rt_ss.at[which, k],
            recv_sem=rt_rs.at[which, k], device_id=(s, (o, o_sib)[which]), device_id_type=MESH,
        )

    for k in SEND_ORDER:
        code_copy(k).start()
    for k, h in PIECES[:AHEAD]:
        block_copy(k, h).start()
    pack(near_base)
    for k in NEAR:
        block_copy(k).start()
    own[d] = send[d]
    forward(0, 1).start()
    forward(0, 0).start()
    for k in NEAR:
        block_copy(k).wait_recv()
        forward(k, 1).start()
        forward(k, 0).start()
    for k in NEAR + CROSS:
        code_copy(k).wait_recv()
    codes[0] = jnp.sum(code_got[...], axis=0)
    codes_copy(0).start()
    codes_copy(1).start()
    loads[2].wait()
    g_own = codes[0]

    def pieces(first, last):
        for i in range(first, last):
            k, h = PIECES[i]
            block_copy(k, h).wait_recv()
            forward(k, 1, h).start()
            if h:
                forward(k, 0).start()
            if i + AHEAD < len(PIECES):
                block_copy(*PIECES[i + AHEAD]).start()

    def partner(g, owner):
        found = jnp.full(g.shape, -1, jnp.int32)
        for c in range(CPD):
            other = pairs[(d * n_owner + owner) * CPD + c] - d * (n_owner * CPD) + 1
            found = jnp.where(g == (owner * CPD + c + 1).astype(jnp.float32), other, found)
        return found.astype(jnp.float32)

    def column(g):
        return jnp.transpose(jnp.broadcast_to(g, (128, slots)))

    p_own = partner(g_own, o)
    columns[0] = column(g_own)
    pieces(0, 2)
    codes_copy(0).wait_recv()
    codes_copy(1).wait_recv()
    p_sib = partner(codes[1], o_sib)
    columns[1] = column(codes[1])
    columns[2] = column(codes[2])
    pieces(2, len(PIECES))

    def table(ref):
        return ref[...].reshape(slots, width)

    def scores(keys, queries):
        return lax.dot_general(keys, queries, NT, preferred_element_type=jnp.float32)

    def wide(column_128):
        return jnp.concatenate([column_128] * (slots // 128), axis=1)

    def masked_max(s, mask):
        return jnp.max(jnp.where(mask, s, -1.0), axis=0, keepdims=True)

    rows_own = table(own)
    key = lax.broadcasted_iota(jnp.int32, (slots, slots), 0)
    query = lax.broadcasted_iota(jnp.int32, (slots, slots), 1)
    best = masked_max(scores(rows_own, rows_own), (wide(columns[0]) == g_own) & (key != query))
    for k in range(n_dp):
        forward(k, 0).wait_recv()
    rows_sib = table(sib)
    best = jnp.maximum(best, masked_max(scores(rows_sib, rows_own), wide(columns[1]) == p_own))
    best_sib = jnp.full((1, slots), -1.0, jnp.float32)

    def neighbour_keys(base):
        keys = cpt[pl.ds(base, half)].reshape(half * cap, width)
        return keys, wide(columns[2, pl.ds(pl.multiple_of(base * cap, half * cap), half * cap)])

    for k in (0,) + NEAR:
        forward(k, 1).wait_recv()
    keys, key_codes = neighbour_keys(near_base)
    best_sib = jnp.maximum(best_sib, masked_max(scores(keys, rows_sib), key_codes == p_sib))
    best = jnp.maximum(best, masked_max(scores(keys, rows_own), key_codes == p_own))
    for k, h in PIECES:
        forward(k, 1, h).wait_recv()
    keys, key_codes = neighbour_keys(cross_base)
    res[1] = jnp.maximum(best_sib, masked_max(scores(keys, rows_sib), key_codes == p_sib))
    for k in (4, 5, 6, 7, 2, 3, 1, 0):
        back(k, 1).start()
    best = jnp.maximum(best, masked_max(scores(keys, rows_own), key_codes == p_own))
    res[0] = best
    for k in SEND_ORDER:
        back(k, 0).start()
    ret[0, d] = best

    for k in range(n_dp):
        back(k, 1).wait_recv()
        if k:
            back(k, 0).wait_recv()
    got = jnp.concatenate([jnp.maximum(ret[0, t], ret[1, t]) for t in range(n_dp)], axis=0)
    picked = lax.dot_general(
        got, lane_hot, (((1,), (0,)), ((), ())),
        preferred_element_type=jnp.float32, precision=lax.Precision.HIGHEST,
    )
    out[...] = jnp.maximum(jnp.sum(t_hot * picked, axis=0, keepdims=True), -1.0)

    for k in (0,) + NEAR + CROSS:
        if k:
            code_copy(k).wait_send()
            back(k, 0).wait_send()
        if k in NEAR:
            block_copy(k).wait_send()
        if k not in CROSS:
            forward(k, 1).wait_send()
        back(k, 1).wait_send()
        forward(k, 0).wait_send()
    for k, h in PIECES:
        block_copy(k, h).wait_send()
        forward(k, 1, h).wait_send()
    codes_copy(0).wait_send()
    codes_copy(1).wait_send()


def fused(embeddings, assignment, pair_list, capacity, n_dp, n_owner):
    rows, width = embeddings.shape
    slots = capacity * n_dp
    block = pltpu.VMEM((n_dp, capacity, width), jnp.bfloat16)
    line = pltpu.VMEM((n_dp, 1, slots), jnp.float32)
    dma = pltpu.SemaphoreType.DMA
    operands = [
        pltpu.with_memory_space_constraint(x, pltpu.HBM)
        for x in (embeddings, assignment.reshape(1, rows), pair_list)
    ]
    best = pl.pallas_call(
        functools.partial(kernel, capacity, n_dp, n_owner),
        out_shape=jax.ShapeDtypeStruct((1, rows), jnp.float32),
        in_specs=[pl.BlockSpec(memory_space=pl.ANY)] * 3,
        out_specs=pl.BlockSpec(memory_space=pltpu.VMEM),
        scratch_shapes=[
            pltpu.VMEM((rows, width), jnp.bfloat16),
            pltpu.VMEM((1, rows), jnp.int32),
            pltpu.SMEM(pair_list.shape, jnp.int32),
            block, block, block, block,
            line, line,
            pltpu.VMEM((3, 1, slots), jnp.float32),
            pltpu.VMEM((3, slots, 128), jnp.float32),
            pltpu.VMEM((2, n_dp, 1, slots), jnp.float32),
            pltpu.VMEM((2, 1, slots), jnp.float32),
            dma((3,)),
            dma((n_dp, 2)), dma((n_dp, 2)), dma((n_dp,)), dma((n_dp,)),
            dma((2, n_dp, 2)), dma((2, n_dp, 2)), dma((2,)), dma((2,)),
            dma((2, n_dp)), dma((2, n_dp)),
        ],
        compiler_params=pltpu.CompilerParams(
            collective_id=0, has_side_effects=True, vmem_limit_bytes=32 * 1024 * 1024
        ),
    )(*operands)
    return best.reshape(rows)


def general(embeddings, assignment, pair_list, capacity, n_dp, n_owner):
    rows, width = embeddings.shape
    slots = capacity * n_dp
    values = embeddings.astype(jnp.float32)
    unit = (values * lax.rsqrt(jnp.sum(values * values, axis=1, keepdims=True) + 1e-06)).astype(
        jnp.bfloat16
    )
    target = assignment // (n_owner * CPD)
    onehot = (target[:, None] == jnp.arange(n_dp, dtype=jnp.int32)[None, :]).astype(jnp.int32)
    slot = jnp.sum(jnp.cumsum(onehot, axis=0) * onehot, axis=1) - 1
    position = target * capacity + slot
    here_owner = lax.axis_index("owner")
    here_dp = lax.axis_index("dp")
    first_id = (here_dp * n_owner + here_owner) * CPD
    partners_mine = lax.dynamic_slice_in_dim(pair_list, first_id, CPD)
    start_best = jnp.full((slots,), -1.0, jnp.float32)
    send_rows = jnp.zeros((slots, width), jnp.bfloat16).at[position].set(unit)
    send_ids = jnp.full((slots,), -1, jnp.int32).at[position].set(assignment)
    got_rows, got_ids = (
        lax.all_to_all(
            send_rows.reshape(n_dp, capacity, width), "dp", split_axis=0, concat_axis=0, tiled=True
        ),
        lax.all_to_all(
            send_ids.reshape(n_dp, capacity), "dp", split_axis=0, concat_axis=0, tiled=True
        ),
    )
    mine = got_rows.reshape(slots, width)
    mine_ids = got_ids.reshape(slots)
    local = jnp.clip(mine_ids - first_id, 0, CPD - 1)
    picked = local[:, None] == jnp.arange(CPD, dtype=jnp.int32)[None, :]
    partner = jnp.sum(jnp.where(picked, partners_mine[None, :], 0), axis=1)
    rows_p = lax.all_gather(mine, "owner", axis=0, tiled=True)
    ids_p = lax.all_gather(mine_ids, "owner", axis=0, tiled=True)
    scores = lax.dot_general(mine, rows_p, NT, preferred_element_type=jnp.float32)
    column = jnp.arange(ids_p.shape[0], dtype=jnp.int32)
    itself = here_owner * slots + jnp.arange(slots, dtype=jnp.int32)
    same = (
        (mine_ids[:, None] == ids_p[None, :])
        & (ids_p[None, :] >= 0)
        & (itself[:, None] != column[None, :])
    )
    related = same | (partner[:, None] == ids_p[None, :])
    best = jnp.maximum(start_best, jnp.max(jnp.where(related, scores, -1.0), axis=1))
    returned = lax.all_to_all(
        best.reshape(n_dp, capacity), "dp", split_axis=0, concat_axis=0, tiled=True
    )
    return returned.reshape(slots)[position]


def shards(embeddings, assignment, pair_list):
    n_dp = lax.axis_size("dp")
    n_owner = lax.axis_size("owner")
    capacity = 2 * embeddings.shape[0] // n_dp
    whole_tiles = n_dp == 8 and n_owner == 4 and capacity % 16 == 0
    form = fused if whole_tiles else general
    return form(embeddings, assignment, pair_list, capacity, n_dp, n_owner)


def solution(mesh):
    placed = (P(("dp", "owner"), None), P(("dp", "owner")), P())
    return jax.shard_map(
        shards, mesh=mesh, in_specs=placed, out_specs=P(("dp", "owner")), check_vma=False
    )
```

```python
import functools

import jax
import jax.numpy as jnp
from jax import lax
from jax.experimental import pallas as pl
from jax.experimental.pallas import tpu as pltpu
from jax.sharding import PartitionSpec as P

CPD = 16
MESH = pl.DeviceIdType.MESH
NT = (((1,), (1,)), ((), ()))


def peer_of(d, k):
    z, y = d // 2, d % 2
    dz, dy = k // 2, k % 2
    if dz == 1:
        z = z + 1 - 2 * (z % 2)
    elif dz == 2:
        z = (z + 2) % 4
    elif dz == 3:
        z = 3 - z
    if dy:
        y = 1 - y
    return z * 2 + y


NEAR = (1, 2, 3)
CROSS = (4, 6, 5, 7)
PIECES = tuple((k, None) for k in CROSS)
AHEAD = 4
SEND_ORDER = (4, 6, 5, 7, 2, 3, 1)


def kernel(
    cap, n_dp, n_owner,
    emb_hbm, asg_hbm, pairs_hbm, out,
    emb, asg, pairs,
    send, own, sib, cpt,
    code_send, code_got, codes, columns, ret, res,
    in_s,
    row_ss, row_rs, id_ss, id_rs, fw_ss, fw_rs, cd_ss, cd_rs, rt_ss, rt_rs,
):
    rows, width = emb.shape
    slots = cap * n_dp
    loads = [
        pltpu.make_async_copy(src, dst, in_s.at[i])
        for i, (src, dst) in enumerate(((asg_hbm, asg), (emb_hbm, emb), (pairs_hbm, pairs)))
    ]
    for load in loads:
        load.start()
    d = lax.axis_index("dp")
    o = lax.axis_index("owner")
    o_sib = o + 1 - 2 * (o % 2)
    o_cpt = (o + 2) % 4
    peers = [peer_of(d, k) for k in range(n_dp)]

    barrier = pltpu.get_barrier_semaphore()
    for k in range(n_dp):
        if k:
            pl.semaphore_signal(barrier, inc=1, device_id=(peers[k], o), device_id_type=MESH)
        pl.semaphore_signal(barrier, inc=1, device_id=(peers[k], o_sib), device_id_type=MESH)
    pl.semaphore_signal(barrier, inc=1, device_id=(d, o_cpt), device_id_type=MESH)

    loads[0].wait()
    a = asg[...]
    t_row = lax.shift_right_logical(a, 6)
    code_row = ((a & 63) + 1).astype(jnp.float32)
    t_hot = (lax.broadcasted_iota(jnp.int32, (n_dp, rows), 0) == t_row).astype(jnp.float32)
    before = (
        lax.broadcasted_iota(jnp.int32, (rows, rows), 0)
        < lax.broadcasted_iota(jnp.int32, (rows, rows), 1)
    ).astype(jnp.float32).astype(jnp.bfloat16)
    count = jnp.dot(t_hot.astype(jnp.bfloat16), before, preferred_element_type=jnp.float32)
    rank = jnp.sum(t_hot * count, axis=0, keepdims=True).astype(jnp.int32)
    slot_iota = lax.broadcasted_iota(jnp.int32, (slots, rows), 0)
    lane_hot = (slot_iota == d * cap + rank).astype(jnp.float32)
    slot_codes = lax.dot_general(
        (t_hot * code_row).astype(jnp.bfloat16),
        lane_hot.astype(jnp.bfloat16),
        NT,
        preferred_element_type=jnp.float32,
    )
    for t in range(n_dp):
        code_send[t] = slot_codes[t : t + 1, :]

    loads[1].wait()
    values = emb[...].astype(jnp.float32)
    unit = (values * lax.rsqrt(jnp.sum(values * values, axis=1, keepdims=True) + 1e-06)).astype(
        jnp.bfloat16
    )
    position = t_row * cap + rank
    half = n_dp // 2
    near_base = (d // half) * half
    cross_base = half - near_base
    group_iota = lax.broadcasted_iota(jnp.int32, (half * cap, rows), 0)

    def pack(base):
        place = (group_iota + base * cap == position).astype(jnp.float32).astype(jnp.bfloat16)
        packed = jnp.dot(place, unit, preferred_element_type=jnp.float32).astype(jnp.bfloat16)
        send[pl.ds(base, half)] = packed.reshape(half, cap, width)

    pack(cross_base)
    code_got[d] = code_send[d]

    pl.semaphore_wait(barrier, 2 * n_dp)

    def part(h):
        return pl.ds(0, cap) if h is None else pl.ds(h * (cap // 2), cap // 2)

    def block_copy(k, h=None):
        p = peers[k]
        return pltpu.make_async_remote_copy(
            src_ref=send.at[p, part(h)], dst_ref=own.at[d, part(h)],
            send_sem=row_ss.at[k, h or 0], recv_sem=row_rs.at[k, h or 0],
            device_id=(p, o), device_id_type=MESH,
        )

    def code_copy(k):
        p = peers[k]
        return pltpu.make_async_remote_copy(
            src_ref=code_send.at[p], dst_ref=code_got.at[d], send_sem=id_ss.at[k],
            recv_sem=id_rs.at[k], device_id=(p, o), device_id_type=MESH,
        )

    def forward(k, which, h=None):
        s = peers[k]
        return pltpu.make_async_remote_copy(
            src_ref=own.at[s, part(h)], dst_ref=(sib, cpt)[which].at[s, part(h)],
            send_sem=fw_ss.at[which, k, h or 0], recv_sem=fw_rs.at[which, k, h or 0],
            device_id=(d, (o_sib, o_cpt)[which]), device_id_type=MESH,
        )

    def codes_copy(which):
        return pltpu.make_async_remote_copy(
            src_ref=codes.at[0], dst_ref=codes.at[1 + which], send_sem=cd_ss.at[which],
            recv_sem=cd_rs.at[which], device_id=(d, (o_sib, o_cpt)[which]), device_id_type=MESH,
        )

    def back(k, which):
        s = peers[k]
        return pltpu.make_async_remote_copy(
            src_ref=res.at[which], dst_ref=ret.at[which, d], send_sem=rt_ss.at[which, k],
            recv_sem=rt_rs.at[which, k], device_id=(s, (o, o_sib)[which]), device_id_type=MESH,
        )

    for k in SEND_ORDER:
        code_copy(k).start()
    for k, h in PIECES[:AHEAD]:
        block_copy(k, h).start()
    pack(near_base)
    for k in NEAR:
        block_copy(k).start()
    own[d] = send[d]
    forward(0, 1).start()
    forward(0, 0).start()
    for k in NEAR:
        block_copy(k).wait_recv()
        forward(k, 1).start()
        forward(k, 0).start()
    for k in NEAR + CROSS:
        code_copy(k).wait_recv()
    codes[0] = jnp.sum(code_got[...], axis=0)
    codes_copy(0).start()
    codes_copy(1).start()
    loads[2].wait()
    g_own = codes[0]

    def pieces(first, last):
        for i in range(first, last):
            k, h = PIECES[i]
            block_copy(k, h).wait_recv()
            forward(k, 1, h).start()
            if h != 0:
                forward(k, 0).start()
            if i + AHEAD < len(PIECES):
                block_copy(*PIECES[i + AHEAD]).start()

    def partner(g, owner):
        found = jnp.full(g.shape, -1, jnp.int32)
        for c in range(CPD):
            other = pairs[(d * n_owner + owner) * CPD + c] - d * (n_owner * CPD) + 1
            found = jnp.where(g == (owner * CPD + c + 1).astype(jnp.float32), other, found)
        return found.astype(jnp.float32)

    def column(g):
        return jnp.transpose(jnp.broadcast_to(g, (128, slots)))

    p_own = partner(g_own, o)
    columns[0] = column(g_own)
    pieces(0, 1)
    codes_copy(0).wait_recv()
    codes_copy(1).wait_recv()
    p_sib = partner(codes[1], o_sib)
    columns[1] = column(codes[1])
    columns[2] = column(codes[2])
    pieces(1, len(PIECES))

    def table(ref):
        return ref[...].reshape(slots, width)

    def scores(keys, queries):
        return lax.dot_general(keys, queries, NT, preferred_element_type=jnp.float32)

    def wide(column_128):
        return jnp.concatenate([column_128] * (slots // 128), axis=1)

    def masked_max(s, mask):
        return jnp.max(jnp.where(mask, s, -1.0), axis=0, keepdims=True)

    rows_own = table(own)
    key = lax.broadcasted_iota(jnp.int32, (slots, slots), 0)
    query = lax.broadcasted_iota(jnp.int32, (slots, slots), 1)
    best = masked_max(scores(rows_own, rows_own), (wide(columns[0]) == g_own) & (key != query))
    for k in range(n_dp):
        forward(k, 0).wait_recv()
    rows_sib = table(sib)
    best = jnp.maximum(best, masked_max(scores(rows_sib, rows_own), wide(columns[1]) == p_own))
    best_sib = jnp.full((1, slots), -1.0, jnp.float32)

    def neighbour_keys(base):
        keys = cpt[pl.ds(base, half)].reshape(half * cap, width)
        return keys, wide(columns[2, pl.ds(pl.multiple_of(base * cap, half * cap), half * cap)])

    for k in (0,) + NEAR:
        forward(k, 1).wait_recv()
    keys, key_codes = neighbour_keys(near_base)
    best_sib = jnp.maximum(best_sib, masked_max(scores(keys, rows_sib), key_codes == p_sib))
    best = jnp.maximum(best, masked_max(scores(keys, rows_own), key_codes == p_own))
    for k, h in PIECES:
        forward(k, 1, h).wait_recv()
    keys, key_codes = neighbour_keys(cross_base)
    res[1] = jnp.maximum(best_sib, masked_max(scores(keys, rows_sib), key_codes == p_sib))
    for k in (4, 5, 6, 7, 2, 3, 1, 0):
        back(k, 1).start()
    best = jnp.maximum(best, masked_max(scores(keys, rows_own), key_codes == p_own))
    res[0] = best
    for k in SEND_ORDER:
        back(k, 0).start()
    ret[0, d] = best

    for k in range(n_dp):
        back(k, 1).wait_recv()
        if k:
            back(k, 0).wait_recv()
    got = jnp.concatenate([jnp.maximum(ret[0, t], ret[1, t]) for t in range(n_dp)], axis=0)
    picked = lax.dot_general(
        got, lane_hot, (((1,), (0,)), ((), ())),
        preferred_element_type=jnp.float32, precision=lax.Precision.HIGHEST,
    )
    out[...] = jnp.maximum(jnp.sum(t_hot * picked, axis=0, keepdims=True), -1.0)

    for k in (0,) + NEAR + CROSS:
        if k:
            code_copy(k).wait_send()
            back(k, 0).wait_send()
        if k in NEAR:
            block_copy(k).wait_send()
        if k not in CROSS:
            forward(k, 1).wait_send()
        back(k, 1).wait_send()
        forward(k, 0).wait_send()
    for k, h in PIECES:
        block_copy(k, h).wait_send()
        forward(k, 1, h).wait_send()
    codes_copy(0).wait_send()
    codes_copy(1).wait_send()


def fused(embeddings, assignment, pair_list, capacity, n_dp, n_owner):
    rows, width = embeddings.shape
    slots = capacity * n_dp
    block = pltpu.VMEM((n_dp, capacity, width), jnp.bfloat16)
    line = pltpu.VMEM((n_dp, 1, slots), jnp.float32)
    dma = pltpu.SemaphoreType.DMA
    operands = [
        pltpu.with_memory_space_constraint(x, pltpu.HBM)
        for x in (embeddings, assignment.reshape(1, rows), pair_list)
    ]
    best = pl.pallas_call(
        functools.partial(kernel, capacity, n_dp, n_owner),
        out_shape=jax.ShapeDtypeStruct((1, rows), jnp.float32),
        in_specs=[pl.BlockSpec(memory_space=pl.ANY)] * 3,
        out_specs=pl.BlockSpec(memory_space=pltpu.VMEM),
        scratch_shapes=[
            pltpu.VMEM((rows, width), jnp.bfloat16),
            pltpu.VMEM((1, rows), jnp.int32),
            pltpu.SMEM(pair_list.shape, jnp.int32),
            block, block, block, block,
            line, line,
            pltpu.VMEM((3, 1, slots), jnp.float32),
            pltpu.VMEM((3, slots, 128), jnp.float32),
            pltpu.VMEM((2, n_dp, 1, slots), jnp.float32),
            pltpu.VMEM((2, 1, slots), jnp.float32),
            dma((3,)),
            dma((n_dp, 2)), dma((n_dp, 2)), dma((n_dp,)), dma((n_dp,)),
            dma((2, n_dp, 2)), dma((2, n_dp, 2)), dma((2,)), dma((2,)),
            dma((2, n_dp)), dma((2, n_dp)),
        ],
        compiler_params=pltpu.CompilerParams(
            collective_id=0, has_side_effects=True, vmem_limit_bytes=32 * 1024 * 1024
        ),
    )(*operands)
    return best.reshape(rows)


def general(embeddings, assignment, pair_list, capacity, n_dp, n_owner):
    rows, width = embeddings.shape
    slots = capacity * n_dp
    values = embeddings.astype(jnp.float32)
    unit = (values * lax.rsqrt(jnp.sum(values * values, axis=1, keepdims=True) + 1e-06)).astype(
        jnp.bfloat16
    )
    target = assignment // (n_owner * CPD)
    onehot = (target[:, None] == jnp.arange(n_dp, dtype=jnp.int32)[None, :]).astype(jnp.int32)
    slot = jnp.sum(jnp.cumsum(onehot, axis=0) * onehot, axis=1) - 1
    position = target * capacity + slot
    here_owner = lax.axis_index("owner")
    here_dp = lax.axis_index("dp")
    first_id = (here_dp * n_owner + here_owner) * CPD
    partners_mine = lax.dynamic_slice_in_dim(pair_list, first_id, CPD)
    start_best = jnp.full((slots,), -1.0, jnp.float32)
    send_rows = jnp.zeros((slots, width), jnp.bfloat16).at[position].set(unit)
    send_ids = jnp.full((slots,), -1, jnp.int32).at[position].set(assignment)
    got_rows, got_ids = (
        lax.all_to_all(
            send_rows.reshape(n_dp, capacity, width), "dp", split_axis=0, concat_axis=0, tiled=True
        ),
        lax.all_to_all(
            send_ids.reshape(n_dp, capacity), "dp", split_axis=0, concat_axis=0, tiled=True
        ),
    )
    mine = got_rows.reshape(slots, width)
    mine_ids = got_ids.reshape(slots)
    local = jnp.clip(mine_ids - first_id, 0, CPD - 1)
    picked = local[:, None] == jnp.arange(CPD, dtype=jnp.int32)[None, :]
    partner = jnp.sum(jnp.where(picked, partners_mine[None, :], 0), axis=1)
    rows_p = lax.all_gather(mine, "owner", axis=0, tiled=True)
    ids_p = lax.all_gather(mine_ids, "owner", axis=0, tiled=True)
    scores = lax.dot_general(mine, rows_p, NT, preferred_element_type=jnp.float32)
    column = jnp.arange(ids_p.shape[0], dtype=jnp.int32)
    itself = here_owner * slots + jnp.arange(slots, dtype=jnp.int32)
    same = (
        (mine_ids[:, None] == ids_p[None, :])
        & (ids_p[None, :] >= 0)
        & (itself[:, None] != column[None, :])
    )
    related = same | (partner[:, None] == ids_p[None, :])
    best = jnp.maximum(start_best, jnp.max(jnp.where(related, scores, -1.0), axis=1))
    returned = lax.all_to_all(
        best.reshape(n_dp, capacity), "dp", split_axis=0, concat_axis=0, tiled=True
    )
    return returned.reshape(slots)[position]


def shards(embeddings, assignment, pair_list):
    n_dp = lax.axis_size("dp")
    n_owner = lax.axis_size("owner")
    capacity = 2 * embeddings.shape[0] // n_dp
    whole_tiles = n_dp == 8 and n_owner == 4 and capacity % 16 == 0
    form = fused if whole_tiles else general
    return form(embeddings, assignment, pair_list, capacity, n_dp, n_owner)


def solution(mesh):
    placed = (P(("dp", "owner"), None), P(("dp", "owner")), P())
    return jax.shard_map(
        shards, mesh=mesh, in_specs=placed, out_specs=P(("dp", "owner")), check_vma=False
    )
```

```python
import functools

import jax
import jax.numpy as jnp
from jax import lax
from jax.experimental import pallas as pl
from jax.experimental.pallas import tpu as pltpu
from jax.sharding import PartitionSpec as P

CPD = 16
MESH = pl.DeviceIdType.MESH
NT = (((1,), (1,)), ((), ()))


def peer_of(d, k):
    z, y = d // 2, d % 2
    dz, dy = k // 2, k % 2
    if dz == 1:
        z = z + 1 - 2 * (z % 2)
    elif dz == 2:
        z = (z + 2) % 4
    elif dz == 3:
        z = 3 - z
    if dy:
        y = 1 - y
    return z * 2 + y


NEAR = (1, 2, 3)
CROSS = (4, 6, 5, 7)
PIECES = tuple((k, None) for k in CROSS)
AHEAD = 4
SEND_ORDER = (4, 6, 5, 7, 2, 3, 1)


def kernel(
    cap, n_dp, n_owner,
    emb_hbm, asg_hbm, pairs_hbm, out,
    emb, asg, pairs,
    send, own, sib, cpt,
    code_send, code_got, codes, columns, ret, res,
    in_s,
    row_ss, row_rs, id_ss, id_rs, fw_ss, fw_rs, cd_ss, cd_rs, rt_ss, rt_rs,
):
    rows, width = emb.shape
    slots = cap * n_dp
    loads = [
        pltpu.make_async_copy(src, dst, in_s.at[i])
        for i, (src, dst) in enumerate(((asg_hbm, asg), (emb_hbm, emb), (pairs_hbm, pairs)))
    ]
    for load in loads:
        load.start()
    d = lax.axis_index("dp")
    o = lax.axis_index("owner")
    o_sib = o + 1 - 2 * (o % 2)
    o_cpt = (o + 2) % 4
    peers = [peer_of(d, k) for k in range(n_dp)]

    barrier = pltpu.get_barrier_semaphore()
    for k in range(n_dp):
        if k:
            pl.semaphore_signal(barrier, inc=1, device_id=(peers[k], o), device_id_type=MESH)
        pl.semaphore_signal(barrier, inc=1, device_id=(peers[k], o_sib), device_id_type=MESH)
    pl.semaphore_signal(barrier, inc=1, device_id=(d, o_cpt), device_id_type=MESH)

    loads[0].wait()
    a = asg[...]
    t_row = lax.shift_right_logical(a, 6)
    code_row = ((a & 63) + 1).astype(jnp.float32)
    t_hot = (lax.broadcasted_iota(jnp.int32, (n_dp, rows), 0) == t_row).astype(jnp.float32)
    before = (
        lax.broadcasted_iota(jnp.int32, (rows, rows), 0)
        < lax.broadcasted_iota(jnp.int32, (rows, rows), 1)
    ).astype(jnp.float32).astype(jnp.bfloat16)
    count = jnp.dot(t_hot.astype(jnp.bfloat16), before, preferred_element_type=jnp.float32)
    rank = jnp.sum(t_hot * count, axis=0, keepdims=True).astype(jnp.int32)
    slot_iota = lax.broadcasted_iota(jnp.int32, (slots, rows), 0)
    lane_hot = (slot_iota == d * cap + rank).astype(jnp.float32)
    slot_codes = lax.dot_general(
        (t_hot * code_row).astype(jnp.bfloat16),
        lane_hot.astype(jnp.bfloat16),
        NT,
        preferred_element_type=jnp.float32,
    )
    for t in range(n_dp):
        code_send[t] = slot_codes[t : t + 1, :]

    loads[1].wait()
    values = emb[...].astype(jnp.float32)
    unit = (values * lax.rsqrt(jnp.sum(values * values, axis=1, keepdims=True) + 1e-06)).astype(
        jnp.bfloat16
    )
    position = t_row * cap + rank
    half = n_dp // 2
    near_base = (d // half) * half
    cross_base = half - near_base
    group_iota = lax.broadcasted_iota(jnp.int32, (half * cap, rows), 0)

    def pack(base):
        place = (group_iota + base * cap == position).astype(jnp.float32).astype(jnp.bfloat16)
        packed = jnp.dot(place, unit, preferred_element_type=jnp.float32).astype(jnp.bfloat16)
        send[pl.ds(base, half)] = packed.reshape(half, cap, width)

    pack(near_base)
    own[d] = send[d]
    code_got[d] = code_send[d]

    pl.semaphore_wait(barrier, 2 * n_dp)

    def part(h):
        return pl.ds(0, cap) if h is None else pl.ds(h * (cap // 2), cap // 2)

    def block_copy(k, h=None):
        p = peers[k]
        return pltpu.make_async_remote_copy(
            src_ref=send.at[p, part(h)], dst_ref=own.at[d, part(h)],
            send_sem=row_ss.at[k, h or 0], recv_sem=row_rs.at[k, h or 0],
            device_id=(p, o), device_id_type=MESH,
        )

    def code_copy(k):
        p = peers[k]
        return pltpu.make_async_remote_copy(
            src_ref=code_send.at[p], dst_ref=code_got.at[d], send_sem=id_ss.at[k],
            recv_sem=id_rs.at[k], device_id=(p, o), device_id_type=MESH,
        )

    def forward(k, which, h=None):
        s = peers[k]
        return pltpu.make_async_remote_copy(
            src_ref=own.at[s, part(h)], dst_ref=(sib, cpt)[which].at[s, part(h)],
            send_sem=fw_ss.at[which, k, h or 0], recv_sem=fw_rs.at[which, k, h or 0],
            device_id=(d, (o_sib, o_cpt)[which]), device_id_type=MESH,
        )

    def codes_copy(which):
        return pltpu.make_async_remote_copy(
            src_ref=codes.at[0], dst_ref=codes.at[1 + which], send_sem=cd_ss.at[which],
            recv_sem=cd_rs.at[which], device_id=(d, (o_sib, o_cpt)[which]), device_id_type=MESH,
        )

    def back(k, which):
        s = peers[k]
        return pltpu.make_async_remote_copy(
            src_ref=res.at[which], dst_ref=ret.at[which, d], send_sem=rt_ss.at[which, k],
            recv_sem=rt_rs.at[which, k], device_id=(s, (o, o_sib)[which]), device_id_type=MESH,
        )

    for k in NEAR:
        block_copy(k).start()
    forward(0, 1).start()
    for k in SEND_ORDER:
        code_copy(k).start()
    pack(cross_base)
    for k, h in PIECES[:2]:
        block_copy(k, h).start()
    for k in NEAR:
        block_copy(k).wait_recv()
        forward(k, 1).start()
        if k > 1:
            block_copy(*PIECES[k]).start()
    for k in (0,) + NEAR:
        forward(k, 0).start()
    for k in NEAR + CROSS:
        code_copy(k).wait_recv()
    codes[0] = jnp.sum(code_got[...], axis=0)
    codes_copy(0).start()
    codes_copy(1).start()
    loads[2].wait()
    g_own = codes[0]

    def pieces(first, last):
        for i in range(first, last):
            k, h = PIECES[i]
            block_copy(k, h).wait_recv()
            forward(k, 1, h).start()
            if h != 0:
                forward(k, 0).start()
            if i + AHEAD < len(PIECES):
                block_copy(*PIECES[i + AHEAD]).start()

    def partner(g, owner):
        found = jnp.full(g.shape, -1, jnp.int32)
        for c in range(CPD):
            other = pairs[(d * n_owner + owner) * CPD + c] - d * (n_owner * CPD) + 1
            found = jnp.where(g == (owner * CPD + c + 1).astype(jnp.float32), other, found)
        return found.astype(jnp.float32)

    def column(g):
        return jnp.transpose(jnp.broadcast_to(g, (128, slots)))

    p_own = partner(g_own, o)
    columns[0] = column(g_own)
    pieces(0, 1)
    codes_copy(0).wait_recv()
    codes_copy(1).wait_recv()
    p_sib = partner(codes[1], o_sib)
    columns[1] = column(codes[1])
    columns[2] = column(codes[2])
    pieces(1, len(PIECES))

    def table(ref):
        return ref[...].reshape(slots, width)

    def scores(keys, queries):
        return lax.dot_general(keys, queries, NT, preferred_element_type=jnp.float32)

    def wide(column_128):
        return jnp.concatenate([column_128] * (slots // 128), axis=1)

    def masked_max(s, mask):
        return jnp.max(jnp.where(mask, s, -1.0), axis=0, keepdims=True)

    rows_own = table(own)
    key = lax.broadcasted_iota(jnp.int32, (slots, slots), 0)
    query = lax.broadcasted_iota(jnp.int32, (slots, slots), 1)
    best = masked_max(scores(rows_own, rows_own), (wide(columns[0]) == g_own) & (key != query))
    for k in range(n_dp):
        forward(k, 0).wait_recv()
    rows_sib = table(sib)
    best = jnp.maximum(best, masked_max(scores(rows_sib, rows_own), wide(columns[1]) == p_own))
    best_sib = jnp.full((1, slots), -1.0, jnp.float32)

    def neighbour_keys(base):
        keys = cpt[pl.ds(base, half)].reshape(half * cap, width)
        return keys, wide(columns[2, pl.ds(pl.multiple_of(base * cap, half * cap), half * cap)])

    for k in (0,) + NEAR:
        forward(k, 1).wait_recv()
    keys, key_codes = neighbour_keys(near_base)
    best_sib = jnp.maximum(best_sib, masked_max(scores(keys, rows_sib), key_codes == p_sib))
    best = jnp.maximum(best, masked_max(scores(keys, rows_own), key_codes == p_own))
    for k, h in PIECES:
        forward(k, 1, h).wait_recv()
    keys, key_codes = neighbour_keys(cross_base)
    res[1] = jnp.maximum(best_sib, masked_max(scores(keys, rows_sib), key_codes == p_sib))
    for k in (4, 5, 6, 7, 2, 3, 1, 0):
        back(k, 1).start()
    best = jnp.maximum(best, masked_max(scores(keys, rows_own), key_codes == p_own))
    res[0] = best
    for k in SEND_ORDER:
        back(k, 0).start()
    ret[0, d] = best

    for k in range(n_dp):
        back(k, 1).wait_recv()
        if k:
            back(k, 0).wait_recv()
    got = jnp.concatenate([jnp.maximum(ret[0, t], ret[1, t]) for t in range(n_dp)], axis=0)
    picked = lax.dot_general(
        got, lane_hot, (((1,), (0,)), ((), ())),
        preferred_element_type=jnp.float32, precision=lax.Precision.HIGHEST,
    )
    out[...] = jnp.maximum(jnp.sum(t_hot * picked, axis=0, keepdims=True), -1.0)

    for k in (0,) + NEAR + CROSS:
        if k:
            code_copy(k).wait_send()
            back(k, 0).wait_send()
        if k in NEAR:
            block_copy(k).wait_send()
        if k not in CROSS:
            forward(k, 1).wait_send()
        back(k, 1).wait_send()
        forward(k, 0).wait_send()
    for k, h in PIECES:
        block_copy(k, h).wait_send()
        forward(k, 1, h).wait_send()
    codes_copy(0).wait_send()
    codes_copy(1).wait_send()


def fused(embeddings, assignment, pair_list, capacity, n_dp, n_owner):
    rows, width = embeddings.shape
    slots = capacity * n_dp
    block = pltpu.VMEM((n_dp, capacity, width), jnp.bfloat16)
    line = pltpu.VMEM((n_dp, 1, slots), jnp.float32)
    dma = pltpu.SemaphoreType.DMA
    operands = [
        pltpu.with_memory_space_constraint(x, pltpu.HBM)
        for x in (embeddings, assignment.reshape(1, rows), pair_list)
    ]
    best = pl.pallas_call(
        functools.partial(kernel, capacity, n_dp, n_owner),
        out_shape=jax.ShapeDtypeStruct((1, rows), jnp.float32),
        in_specs=[pl.BlockSpec(memory_space=pl.ANY)] * 3,
        out_specs=pl.BlockSpec(memory_space=pltpu.VMEM),
        scratch_shapes=[
            pltpu.VMEM((rows, width), jnp.bfloat16),
            pltpu.VMEM((1, rows), jnp.int32),
            pltpu.SMEM(pair_list.shape, jnp.int32),
            block, block, block, block,
            line, line,
            pltpu.VMEM((3, 1, slots), jnp.float32),
            pltpu.VMEM((3, slots, 128), jnp.float32),
            pltpu.VMEM((2, n_dp, 1, slots), jnp.float32),
            pltpu.VMEM((2, 1, slots), jnp.float32),
            dma((3,)),
            dma((n_dp, 2)), dma((n_dp, 2)), dma((n_dp,)), dma((n_dp,)),
            dma((2, n_dp, 2)), dma((2, n_dp, 2)), dma((2,)), dma((2,)),
            dma((2, n_dp)), dma((2, n_dp)),
        ],
        compiler_params=pltpu.CompilerParams(
            collective_id=0, has_side_effects=True, vmem_limit_bytes=32 * 1024 * 1024
        ),
    )(*operands)
    return best.reshape(rows)


def general(embeddings, assignment, pair_list, capacity, n_dp, n_owner):
    rows, width = embeddings.shape
    slots = capacity * n_dp
    values = embeddings.astype(jnp.float32)
    unit = (values * lax.rsqrt(jnp.sum(values * values, axis=1, keepdims=True) + 1e-06)).astype(
        jnp.bfloat16
    )
    target = assignment // (n_owner * CPD)
    onehot = (target[:, None] == jnp.arange(n_dp, dtype=jnp.int32)[None, :]).astype(jnp.int32)
    slot = jnp.sum(jnp.cumsum(onehot, axis=0) * onehot, axis=1) - 1
    position = target * capacity + slot
    here_owner = lax.axis_index("owner")
    here_dp = lax.axis_index("dp")
    first_id = (here_dp * n_owner + here_owner) * CPD
    partners_mine = lax.dynamic_slice_in_dim(pair_list, first_id, CPD)
    start_best = jnp.full((slots,), -1.0, jnp.float32)
    send_rows = jnp.zeros((slots, width), jnp.bfloat16).at[position].set(unit)
    send_ids = jnp.full((slots,), -1, jnp.int32).at[position].set(assignment)
    got_rows, got_ids = (
        lax.all_to_all(
            send_rows.reshape(n_dp, capacity, width), "dp", split_axis=0, concat_axis=0, tiled=True
        ),
        lax.all_to_all(
            send_ids.reshape(n_dp, capacity), "dp", split_axis=0, concat_axis=0, tiled=True
        ),
    )
    mine = got_rows.reshape(slots, width)
    mine_ids = got_ids.reshape(slots)
    local = jnp.clip(mine_ids - first_id, 0, CPD - 1)
    picked = local[:, None] == jnp.arange(CPD, dtype=jnp.int32)[None, :]
    partner = jnp.sum(jnp.where(picked, partners_mine[None, :], 0), axis=1)
    rows_p = lax.all_gather(mine, "owner", axis=0, tiled=True)
    ids_p = lax.all_gather(mine_ids, "owner", axis=0, tiled=True)
    scores = lax.dot_general(mine, rows_p, NT, preferred_element_type=jnp.float32)
    column = jnp.arange(ids_p.shape[0], dtype=jnp.int32)
    itself = here_owner * slots + jnp.arange(slots, dtype=jnp.int32)
    same = (
        (mine_ids[:, None] == ids_p[None, :])
        & (ids_p[None, :] >= 0)
        & (itself[:, None] != column[None, :])
    )
    related = same | (partner[:, None] == ids_p[None, :])
    best = jnp.maximum(start_best, jnp.max(jnp.where(related, scores, -1.0), axis=1))
    returned = lax.all_to_all(
        best.reshape(n_dp, capacity), "dp", split_axis=0, concat_axis=0, tiled=True
    )
    return returned.reshape(slots)[position]


def shards(embeddings, assignment, pair_list):
    n_dp = lax.axis_size("dp")
    n_owner = lax.axis_size("owner")
    capacity = 2 * embeddings.shape[0] // n_dp
    whole_tiles = n_dp == 8 and n_owner == 4 and capacity % 16 == 0
    form = fused if whole_tiles else general
    return form(embeddings, assignment, pair_list, capacity, n_dp, n_owner)


def solution(mesh):
    placed = (P(("dp", "owner"), None), P(("dp", "owner")), P())
    return jax.shard_map(
        shards, mesh=mesh, in_specs=placed, out_specs=P(("dp", "owner")), check_vma=False
    )
```

```python
import functools

import jax
import jax.numpy as jnp
from jax import lax
from jax.experimental import pallas as pl
from jax.experimental.pallas import tpu as pltpu
from jax.sharding import PartitionSpec as P

CPD = 16
MESH = pl.DeviceIdType.MESH
NT = (((1,), (1,)), ((), ()))


def peer_of(d, k):
    z, y = d // 2, d % 2
    dz, dy = k // 2, k % 2
    if dz == 1:
        z = z + 1 - 2 * (z % 2)
    elif dz == 2:
        z = (z + 2) % 4
    elif dz == 3:
        z = 3 - z
    if dy:
        y = 1 - y
    return z * 2 + y


NEAR = (1, 2, 3)
CROSS = (4, 6, 5, 7)
SEND_ORDER = (4, 6, 5, 7, 2, 3, 1)


def kernel(
    cap, n_dp, n_owner,
    emb_hbm, asg_hbm, pairs_hbm, out,
    emb, asg, pairs,
    send, own, sib, cpt,
    code_send, code_got, codes, columns, ret, res,
    in_s,
    row_ss, row_rs, id_ss, id_rs, fw_ss, fw_rs, cd_ss, cd_rs, rt_ss, rt_rs,
):
    rows, width = emb.shape
    slots = cap * n_dp
    loads = [
        pltpu.make_async_copy(src, dst, in_s.at[i])
        for i, (src, dst) in enumerate(((asg_hbm, asg), (emb_hbm, emb), (pairs_hbm, pairs)))
    ]
    for load in loads:
        load.start()
    d = lax.axis_index("dp")
    o = lax.axis_index("owner")
    o_sib = o + 1 - 2 * (o % 2)
    o_cpt = (o + 2) % 4
    peers = [peer_of(d, k) for k in range(n_dp)]

    barrier = pltpu.get_barrier_semaphore()
    for k in range(n_dp):
        if k:
            pl.semaphore_signal(barrier, inc=1, device_id=(peers[k], o), device_id_type=MESH)
        pl.semaphore_signal(barrier, inc=1, device_id=(peers[k], o_sib), device_id_type=MESH)
    pl.semaphore_signal(barrier, inc=1, device_id=(d, o_cpt), device_id_type=MESH)

    loads[0].wait()
    a = asg[...]
    t_row = lax.shift_right_logical(a, 6)
    code_row = ((a & 63) + 1).astype(jnp.float32)
    t_hot = (lax.broadcasted_iota(jnp.int32, (n_dp, rows), 0) == t_row).astype(jnp.float32)
    before = (
        lax.broadcasted_iota(jnp.int32, (rows, rows), 0)
        < lax.broadcasted_iota(jnp.int32, (rows, rows), 1)
    ).astype(jnp.float32).astype(jnp.bfloat16)
    count = jnp.dot(t_hot.astype(jnp.bfloat16), before, preferred_element_type=jnp.float32)
    rank = jnp.sum(t_hot * count, axis=0, keepdims=True).astype(jnp.int32)
    slot_iota = lax.broadcasted_iota(jnp.int32, (slots, rows), 0)
    lane_hot = (slot_iota == d * cap + rank).astype(jnp.float32)
    slot_codes = lax.dot_general(
        (t_hot * code_row).astype(jnp.bfloat16),
        lane_hot.astype(jnp.bfloat16),
        NT,
        preferred_element_type=jnp.float32,
    )
    for t in range(n_dp):
        code_send[t] = slot_codes[t : t + 1, :]

    loads[1].wait()
    values = emb[...].astype(jnp.float32)
    unit = (values * lax.rsqrt(jnp.sum(values * values, axis=1, keepdims=True) + 1e-06)).astype(
        jnp.bfloat16
    )
    position = t_row * cap + rank
    half = n_dp // 2
    near_base = (d // half) * half
    cross_base = half - near_base
    group_iota = lax.broadcasted_iota(jnp.int32, (half * cap, rows), 0)

    def pack(base):
        place = (group_iota + base * cap == position).astype(jnp.float32).astype(jnp.bfloat16)
        packed = jnp.dot(place, unit, preferred_element_type=jnp.float32).astype(jnp.bfloat16)
        send[pl.ds(base, half)] = packed.reshape(half, cap, width)

    pack(near_base)
    pack(cross_base)
    own[d] = send[d]
    code_got[d] = code_send[d]

    pl.semaphore_wait(barrier, 2 * n_dp)

    def block_copy(k):
        p = peers[k]
        return pltpu.make_async_remote_copy(
            src_ref=send.at[p], dst_ref=own.at[d],
            send_sem=row_ss.at[k], recv_sem=row_rs.at[k],
            device_id=(p, o), device_id_type=MESH,
        )

    def code_copy(k):
        p = peers[k]
        return pltpu.make_async_remote_copy(
            src_ref=code_send.at[p], dst_ref=code_got.at[d], send_sem=id_ss.at[k],
            recv_sem=id_rs.at[k], device_id=(p, o), device_id_type=MESH,
        )

    def forward(k, which):
        s = peers[k]
        return pltpu.make_async_remote_copy(
            src_ref=own.at[s], dst_ref=(sib, cpt)[which].at[s],
            send_sem=fw_ss.at[which, k], recv_sem=fw_rs.at[which, k],
            device_id=(d, (o_sib, o_cpt)[which]), device_id_type=MESH,
        )

    def codes_copy(which):
        return pltpu.make_async_remote_copy(
            src_ref=codes.at[0], dst_ref=codes.at[1 + which], send_sem=cd_ss.at[which],
            recv_sem=cd_rs.at[which], device_id=(d, (o_sib, o_cpt)[which]), device_id_type=MESH,
        )

    def back(k, which):
        s = peers[k]
        return pltpu.make_async_remote_copy(
            src_ref=res.at[which], dst_ref=ret.at[which, d], send_sem=rt_ss.at[which, k],
            recv_sem=rt_rs.at[which, k], device_id=(s, (o, o_sib)[which]), device_id_type=MESH,
        )

    def pass_on(ks):
        for k in ks:
            block_copy(k).wait_recv()
            forward(k, 1).start()

    def send_codes():
        for k in SEND_ORDER:
            code_copy(k).start()

    first_core = o % 2 == 0
    second_core = o % 2 == 1

    @pl.when(first_core)
    def _():
        send_codes()
        for k in CROSS + NEAR:
            block_copy(k).start()
        forward(0, 1).start()
        pass_on(CROSS[:2])

    @pl.when(second_core)
    def _():
        for k in NEAR:
            block_copy(k).start()
        forward(0, 1).start()
        send_codes()
        pass_on(NEAR)
        for k in CROSS:
            block_copy(k).start()

    for k in NEAR + CROSS:
        code_copy(k).wait_recv()
    codes[0] = jnp.sum(code_got[...], axis=0)
    codes_copy(0).start()
    codes_copy(1).start()
    loads[2].wait()
    g_own = codes[0]

    def partner(g, owner):
        found = jnp.full(g.shape, -1, jnp.int32)
        for c in range(CPD):
            other = pairs[(d * n_owner + owner) * CPD + c] - d * (n_owner * CPD) + 1
            found = jnp.where(g == (owner * CPD + c + 1).astype(jnp.float32), other, found)
        return found.astype(jnp.float32)

    def column(g):
        return jnp.transpose(jnp.broadcast_to(g, (128, slots)))

    p_own = partner(g_own, o)
    columns[0] = column(g_own)

    @pl.when(first_core)
    def _():
        pass_on(CROSS[2:] + NEAR)
        for k in CROSS + (0,) + NEAR:
            forward(k, 0).start()

    @pl.when(second_core)
    def _():
        for k in (0,) + NEAR:
            forward(k, 0).start()
        for k in CROSS:
            pass_on((k,))
            forward(k, 0).start()

    codes_copy(0).wait_recv()
    codes_copy(1).wait_recv()
    p_sib = partner(codes[1], o_sib)
    columns[1] = column(codes[1])
    columns[2] = column(codes[2])

    def table(ref):
        return ref[...].reshape(slots, width)

    def scores(keys, queries):
        return lax.dot_general(keys, queries, NT, preferred_element_type=jnp.float32)

    def wide(column_128):
        return jnp.concatenate([column_128] * (slots // 128), axis=1)

    def masked_max(s, mask):
        return jnp.max(jnp.where(mask, s, -1.0), axis=0, keepdims=True)

    rows_own = table(own)
    key = lax.broadcasted_iota(jnp.int32, (slots, slots), 0)
    query = lax.broadcasted_iota(jnp.int32, (slots, slots), 1)
    best = masked_max(scores(rows_own, rows_own), (wide(columns[0]) == g_own) & (key != query))
    for k in range(n_dp):
        forward(k, 0).wait_recv()
    rows_sib = table(sib)
    best = jnp.maximum(best, masked_max(scores(rows_sib, rows_own), wide(columns[1]) == p_own))
    best_sib = jnp.full((1, slots), -1.0, jnp.float32)

    def neighbour_keys(base):
        keys = cpt[pl.ds(base, half)].reshape(half * cap, width)
        return keys, wide(columns[2, pl.ds(pl.multiple_of(base * cap, half * cap), half * cap)])

    def arrived(ks):
        for k in ks:
            forward(k, 1).wait_recv()

    pl.when(first_core)(lambda: arrived(CROSS))
    pl.when(second_core)(lambda: arrived((0,) + NEAR))
    early_base = (1 - o % 2) * cross_base + (o % 2) * near_base
    keys, key_codes = neighbour_keys(early_base)
    best_sib = jnp.maximum(best_sib, masked_max(scores(keys, rows_sib), key_codes == p_sib))
    best = jnp.maximum(best, masked_max(scores(keys, rows_own), key_codes == p_own))
    pl.when(first_core)(lambda: arrived((0,) + NEAR))
    pl.when(second_core)(lambda: arrived(CROSS))
    keys, key_codes = neighbour_keys(half - early_base)
    res[1] = jnp.maximum(best_sib, masked_max(scores(keys, rows_sib), key_codes == p_sib))
    for k in (4, 5, 6, 7, 2, 3, 1, 0):
        back(k, 1).start()
    best = jnp.maximum(best, masked_max(scores(keys, rows_own), key_codes == p_own))
    res[0] = best
    for k in SEND_ORDER:
        back(k, 0).start()
    ret[0, d] = best

    for k in range(n_dp):
        back(k, 1).wait_recv()
        if k:
            back(k, 0).wait_recv()
    got = jnp.concatenate([jnp.maximum(ret[0, t], ret[1, t]) for t in range(n_dp)], axis=0)
    picked = lax.dot_general(
        got, lane_hot, (((1,), (0,)), ((), ())),
        preferred_element_type=jnp.float32, precision=lax.Precision.HIGHEST,
    )
    out[...] = jnp.maximum(jnp.sum(t_hot * picked, axis=0, keepdims=True), -1.0)

    for k in (0,) + NEAR + CROSS:
        if k:
            code_copy(k).wait_send()
            back(k, 0).wait_send()
            block_copy(k).wait_send()
        forward(k, 1).wait_send()
        back(k, 1).wait_send()
        forward(k, 0).wait_send()
    codes_copy(0).wait_send()
    codes_copy(1).wait_send()


def fused(embeddings, assignment, pair_list, capacity, n_dp, n_owner):
    rows, width = embeddings.shape
    slots = capacity * n_dp
    block = pltpu.VMEM((n_dp, capacity, width), jnp.bfloat16)
    line = pltpu.VMEM((n_dp, 1, slots), jnp.float32)
    dma = pltpu.SemaphoreType.DMA
    operands = [
        pltpu.with_memory_space_constraint(x, pltpu.HBM)
        for x in (embeddings, assignment.reshape(1, rows), pair_list)
    ]
    best = pl.pallas_call(
        functools.partial(kernel, capacity, n_dp, n_owner),
        out_shape=jax.ShapeDtypeStruct((1, rows), jnp.float32),
        in_specs=[pl.BlockSpec(memory_space=pl.ANY)] * 3,
        out_specs=pl.BlockSpec(memory_space=pltpu.VMEM),
        scratch_shapes=[
            pltpu.VMEM((rows, width), jnp.bfloat16),
            pltpu.VMEM((1, rows), jnp.int32),
            pltpu.SMEM(pair_list.shape, jnp.int32),
            block, block, block, block,
            line, line,
            pltpu.VMEM((3, 1, slots), jnp.float32),
            pltpu.VMEM((3, slots, 128), jnp.float32),
            pltpu.VMEM((2, n_dp, 1, slots), jnp.float32),
            pltpu.VMEM((2, 1, slots), jnp.float32),
            dma((3,)),
            dma((n_dp,)), dma((n_dp,)), dma((n_dp,)), dma((n_dp,)),
            dma((2, n_dp)), dma((2, n_dp)), dma((2,)), dma((2,)),
            dma((2, n_dp)), dma((2, n_dp)),
        ],
        compiler_params=pltpu.CompilerParams(
            collective_id=0, has_side_effects=True, vmem_limit_bytes=32 * 1024 * 1024
        ),
    )(*operands)
    return best.reshape(rows)


def general(embeddings, assignment, pair_list, capacity, n_dp, n_owner):
    rows, width = embeddings.shape
    slots = capacity * n_dp
    values = embeddings.astype(jnp.float32)
    unit = (values * lax.rsqrt(jnp.sum(values * values, axis=1, keepdims=True) + 1e-06)).astype(
        jnp.bfloat16
    )
    target = assignment // (n_owner * CPD)
    onehot = (target[:, None] == jnp.arange(n_dp, dtype=jnp.int32)[None, :]).astype(jnp.int32)
    slot = jnp.sum(jnp.cumsum(onehot, axis=0) * onehot, axis=1) - 1
    position = target * capacity + slot
    here_owner = lax.axis_index("owner")
    here_dp = lax.axis_index("dp")
    first_id = (here_dp * n_owner + here_owner) * CPD
    partners_mine = lax.dynamic_slice_in_dim(pair_list, first_id, CPD)
    start_best = jnp.full((slots,), -1.0, jnp.float32)
    send_rows = jnp.zeros((slots, width), jnp.bfloat16).at[position].set(unit)
    send_ids = jnp.full((slots,), -1, jnp.int32).at[position].set(assignment)
    got_rows, got_ids = (
        lax.all_to_all(
            send_rows.reshape(n_dp, capacity, width), "dp", split_axis=0, concat_axis=0, tiled=True
        ),
        lax.all_to_all(
            send_ids.reshape(n_dp, capacity), "dp", split_axis=0, concat_axis=0, tiled=True
        ),
    )
    mine = got_rows.reshape(slots, width)
    mine_ids = got_ids.reshape(slots)
    local = jnp.clip(mine_ids - first_id, 0, CPD - 1)
    picked = local[:, None] == jnp.arange(CPD, dtype=jnp.int32)[None, :]
    partner = jnp.sum(jnp.where(picked, partners_mine[None, :], 0), axis=1)
    rows_p = lax.all_gather(mine, "owner", axis=0, tiled=True)
    ids_p = lax.all_gather(mine_ids, "owner", axis=0, tiled=True)
    scores = lax.dot_general(mine, rows_p, NT, preferred_element_type=jnp.float32)
    column = jnp.arange(ids_p.shape[0], dtype=jnp.int32)
    itself = here_owner * slots + jnp.arange(slots, dtype=jnp.int32)
    same = (
        (mine_ids[:, None] == ids_p[None, :])
        & (ids_p[None, :] >= 0)
        & (itself[:, None] != column[None, :])
    )
    related = same | (partner[:, None] == ids_p[None, :])
    best = jnp.maximum(start_best, jnp.max(jnp.where(related, scores, -1.0), axis=1))
    returned = lax.all_to_all(
        best.reshape(n_dp, capacity), "dp", split_axis=0, concat_axis=0, tiled=True
    )
    return returned.reshape(slots)[position]


def shards(embeddings, assignment, pair_list):
    n_dp = lax.axis_size("dp")
    n_owner = lax.axis_size("owner")
    capacity = 2 * embeddings.shape[0] // n_dp
    whole_tiles = n_dp == 8 and n_owner == 4 and capacity % 16 == 0
    form = fused if whole_tiles else general
    return form(embeddings, assignment, pair_list, capacity, n_dp, n_owner)


def solution(mesh):
    placed = (P(("dp", "owner"), None), P(("dp", "owner")), P())
    return jax.shard_map(
        shards, mesh=mesh, in_specs=placed, out_specs=P(("dp", "owner")), check_vma=False
    )
```

```python
import functools

import jax
import jax.numpy as jnp
from jax import lax
from jax.experimental import pallas as pl
from jax.experimental.pallas import tpu as pltpu
from jax.sharding import PartitionSpec as P

CPD = 16
MESH = pl.DeviceIdType.MESH
NT = (((1,), (1,)), ((), ()))


def peer_of(d, k):
    z, y = d // 2, d % 2
    dz, dy = k // 2, k % 2
    if dz == 1:
        z = z + 1 - 2 * (z % 2)
    elif dz == 2:
        z = (z + 2) % 4
    elif dz == 3:
        z = 3 - z
    if dy:
        y = 1 - y
    return z * 2 + y


NEAR = (1, 2, 3)
CROSS = (4, 6, 5, 7)
PIECES = tuple((k, None) for k in CROSS)
AHEAD = 3
SEND_ORDER = (4, 6, 5, 7, 2, 3, 1)


def kernel(
    cap, n_dp, n_owner,
    emb_hbm, asg_hbm, pairs_hbm, out,
    emb, asg, pairs,
    send, own, sib, cpt,
    code_send, code_got, codes, columns, ret, res,
    in_s,
    row_ss, row_rs, id_ss, id_rs, fw_ss, fw_rs, cd_ss, cd_rs, rt_ss, rt_rs,
):
    rows, width = emb.shape
    slots = cap * n_dp
    loads = [
        pltpu.make_async_copy(src, dst, in_s.at[i])
        for i, (src, dst) in enumerate(((asg_hbm, asg), (emb_hbm, emb), (pairs_hbm, pairs)))
    ]
    for load in loads:
        load.start()
    d = lax.axis_index("dp")
    o = lax.axis_index("owner")
    o_sib = o + 1 - 2 * (o % 2)
    o_cpt = (o + 2) % 4
    peers = [peer_of(d, k) for k in range(n_dp)]

    barrier = pltpu.get_barrier_semaphore()
    for k in range(n_dp):
        if k:
            pl.semaphore_signal(barrier, inc=1, device_id=(peers[k], o), device_id_type=MESH)
        pl.semaphore_signal(barrier, inc=1, device_id=(peers[k], o_sib), device_id_type=MESH)
    pl.semaphore_signal(barrier, inc=1, device_id=(d, o_cpt), device_id_type=MESH)

    loads[0].wait()
    a = asg[...]
    t_row = lax.shift_right_logical(a, 6)
    code_row = ((a & 63) + 1).astype(jnp.float32)
    t_hot = (lax.broadcasted_iota(jnp.int32, (n_dp, rows), 0) == t_row).astype(jnp.float32)
    before = (
        lax.broadcasted_iota(jnp.int32, (rows, rows), 0)
        < lax.broadcasted_iota(jnp.int32, (rows, rows), 1)
    ).astype(jnp.float32).astype(jnp.bfloat16)
    count = jnp.dot(t_hot.astype(jnp.bfloat16), before, preferred_element_type=jnp.float32)
    rank = jnp.sum(t_hot * count, axis=0, keepdims=True).astype(jnp.int32)
    slot_iota = lax.broadcasted_iota(jnp.int32, (slots, rows), 0)
    lane_hot = (slot_iota == d * cap + rank).astype(jnp.float32)
    slot_codes = lax.dot_general(
        (t_hot * code_row).astype(jnp.bfloat16),
        lane_hot.astype(jnp.bfloat16),
        NT,
        preferred_element_type=jnp.float32,
    )
    for t in range(n_dp):
        code_send[t] = slot_codes[t : t + 1, :]

    loads[1].wait()
    values = emb[...].astype(jnp.float32)
    unit = (values * lax.rsqrt(jnp.sum(values * values, axis=1, keepdims=True) + 1e-06)).astype(
        jnp.bfloat16
    )
    position = t_row * cap + rank
    half = n_dp // 2
    near_base = (d // half) * half
    cross_base = half - near_base
    group_iota = lax.broadcasted_iota(jnp.int32, (half * cap, rows), 0)

    def pack(base):
        place = (group_iota + base * cap == position).astype(jnp.float32).astype(jnp.bfloat16)
        packed = jnp.dot(place, unit, preferred_element_type=jnp.float32).astype(jnp.bfloat16)
        send[pl.ds(base, half)] = packed.reshape(half, cap, width)

    pack(near_base)
    own[d] = send[d]
    code_got[d] = code_send[d]

    pl.semaphore_wait(barrier, 2 * n_dp)

    def part(h):
        return pl.ds(0, cap) if h is None else pl.ds(h * (cap // 2), cap // 2)

    def block_copy(k, h=None):
        p = peers[k]
        return pltpu.make_async_remote_copy(
            src_ref=send.at[p, part(h)], dst_ref=own.at[d, part(h)],
            send_sem=row_ss.at[k, h or 0], recv_sem=row_rs.at[k, h or 0],
            device_id=(p, o), device_id_type=MESH,
        )

    def code_copy(k):
        p = peers[k]
        return pltpu.make_async_remote_copy(
            src_ref=code_send.at[p], dst_ref=code_got.at[d], send_sem=id_ss.at[k],
            recv_sem=id_rs.at[k], device_id=(p, o), device_id_type=MESH,
        )

    def forward(k, which, h=None):
        s = peers[k]
        return pltpu.make_async_remote_copy(
            src_ref=own.at[s, part(h)], dst_ref=(sib, cpt)[which].at[s, part(h)],
            send_sem=fw_ss.at[which, k, h or 0], recv_sem=fw_rs.at[which, k, h or 0],
            device_id=(d, (o_sib, o_cpt)[which]), device_id_type=MESH,
        )

    def codes_copy(which):
        return pltpu.make_async_remote_copy(
            src_ref=codes.at[0], dst_ref=codes.at[1 + which], send_sem=cd_ss.at[which],
            recv_sem=cd_rs.at[which], device_id=(d, (o_sib, o_cpt)[which]), device_id_type=MESH,
        )

    def back(k, which):
        s = peers[k]
        return pltpu.make_async_remote_copy(
            src_ref=res.at[which], dst_ref=ret.at[which, d], send_sem=rt_ss.at[which, k],
            recv_sem=rt_rs.at[which, k], device_id=(s, (o, o_sib)[which]), device_id_type=MESH,
        )

    for k in NEAR:
        block_copy(k).start()
    forward(0, 1).start()
    for k in SEND_ORDER:
        code_copy(k).start()
    pack(cross_base)
    for k, h in PIECES[:2]:
        block_copy(k, h).start()
    for k in NEAR:
        block_copy(k).wait_recv()
        forward(k, 1).start()
        if k == 2:
            block_copy(*PIECES[2]).start()
    for k in (0,) + NEAR:
        forward(k, 0).start()
    for k in NEAR + CROSS:
        code_copy(k).wait_recv()
    codes[0] = jnp.sum(code_got[...], axis=0)
    codes_copy(0).start()
    codes_copy(1).start()
    loads[2].wait()
    g_own = codes[0]

    def pieces(first, last):
        for i in range(first, last):
            k, h = PIECES[i]
            block_copy(k, h).wait_recv()
            forward(k, 1, h).start()
            if h != 0:
                forward(k, 0).start()
            if i + AHEAD < len(PIECES):
                block_copy(*PIECES[i + AHEAD]).start()

    def partner(g, owner):
        found = jnp.full(g.shape, -1, jnp.int32)
        for c in range(CPD):
            other = pairs[(d * n_owner + owner) * CPD + c] - d * (n_owner * CPD) + 1
            found = jnp.where(g == (owner * CPD + c + 1).astype(jnp.float32), other, found)
        return found.astype(jnp.float32)

    def column(g):
        return jnp.transpose(jnp.broadcast_to(g, (128, slots)))

    p_own = partner(g_own, o)
    columns[0] = column(g_own)
    pieces(0, 1)
    codes_copy(0).wait_recv()
    codes_copy(1).wait_recv()
    p_sib = partner(codes[1], o_sib)
    columns[1] = column(codes[1])
    columns[2] = column(codes[2])
    pieces(1, len(PIECES))

    def table(ref):
        return ref[...].reshape(slots, width)

    def scores(keys, queries):
        return lax.dot_general(keys, queries, NT, preferred_element_type=jnp.float32)

    def wide(column_128):
        return jnp.concatenate([column_128] * (slots // 128), axis=1)

    def masked_max(s, mask):
        return jnp.max(jnp.where(mask, s, -1.0), axis=0, keepdims=True)

    rows_own = table(own)
    key = lax.broadcasted_iota(jnp.int32, (slots, slots), 0)
    query = lax.broadcasted_iota(jnp.int32, (slots, slots), 1)
    best = masked_max(scores(rows_own, rows_own), (wide(columns[0]) == g_own) & (key != query))
    for k in range(n_dp):
        forward(k, 0).wait_recv()
    rows_sib = table(sib)
    best = jnp.maximum(best, masked_max(scores(rows_sib, rows_own), wide(columns[1]) == p_own))
    best_sib = jnp.full((1, slots), -1.0, jnp.float32)

    def neighbour_keys(base):
        keys = cpt[pl.ds(base, half)].reshape(half * cap, width)
        return keys, wide(columns[2, pl.ds(pl.multiple_of(base * cap, half * cap), half * cap)])

    for k in (0,) + NEAR:
        forward(k, 1).wait_recv()
    keys, key_codes = neighbour_keys(near_base)
    best_sib = jnp.maximum(best_sib, masked_max(scores(keys, rows_sib), key_codes == p_sib))
    best = jnp.maximum(best, masked_max(scores(keys, rows_own), key_codes == p_own))
    for k, h in PIECES:
        forward(k, 1, h).wait_recv()
    keys, key_codes = neighbour_keys(cross_base)
    res[1] = jnp.maximum(best_sib, masked_max(scores(keys, rows_sib), key_codes == p_sib))
    for k in (4, 5, 6, 7, 2, 3, 1, 0):
        back(k, 1).start()
    best = jnp.maximum(best, masked_max(scores(keys, rows_own), key_codes == p_own))
    res[0] = best
    for k in SEND_ORDER:
        back(k, 0).start()
    ret[0, d] = best

    for k in range(n_dp):
        back(k, 1).wait_recv()
        if k:
            back(k, 0).wait_recv()
    got = jnp.concatenate([jnp.maximum(ret[0, t], ret[1, t]) for t in range(n_dp)], axis=0)
    picked = lax.dot_general(
        got, lane_hot, (((1,), (0,)), ((), ())),
        preferred_element_type=jnp.float32, precision=lax.Precision.HIGHEST,
    )
    out[...] = jnp.maximum(jnp.sum(t_hot * picked, axis=0, keepdims=True), -1.0)

    for k in (0,) + NEAR + CROSS:
        if k:
            code_copy(k).wait_send()
            back(k, 0).wait_send()
        if k in NEAR:
            block_copy(k).wait_send()
        if k not in CROSS:
            forward(k, 1).wait_send()
        back(k, 1).wait_send()
        forward(k, 0).wait_send()
    for k, h in PIECES:
        block_copy(k, h).wait_send()
        forward(k, 1, h).wait_send()
    codes_copy(0).wait_send()
    codes_copy(1).wait_send()


def fused(embeddings, assignment, pair_list, capacity, n_dp, n_owner):
    rows, width = embeddings.shape
    slots = capacity * n_dp
    block = pltpu.VMEM((n_dp, capacity, width), jnp.bfloat16)
    line = pltpu.VMEM((n_dp, 1, slots), jnp.float32)
    dma = pltpu.SemaphoreType.DMA
    operands = [
        pltpu.with_memory_space_constraint(x, pltpu.HBM)
        for x in (embeddings, assignment.reshape(1, rows), pair_list)
    ]
    best = pl.pallas_call(
        functools.partial(kernel, capacity, n_dp, n_owner),
        out_shape=jax.ShapeDtypeStruct((1, rows), jnp.float32),
        in_specs=[pl.BlockSpec(memory_space=pl.ANY)] * 3,
        out_specs=pl.BlockSpec(memory_space=pltpu.VMEM),
        scratch_shapes=[
            pltpu.VMEM((rows, width), jnp.bfloat16),
            pltpu.VMEM((1, rows), jnp.int32),
            pltpu.SMEM(pair_list.shape, jnp.int32),
            block, block, block, block,
            line, line,
            pltpu.VMEM((3, 1, slots), jnp.float32),
            pltpu.VMEM((3, slots, 128), jnp.float32),
            pltpu.VMEM((2, n_dp, 1, slots), jnp.float32),
            pltpu.VMEM((2, 1, slots), jnp.float32),
            dma((3,)),
            dma((n_dp, 2)), dma((n_dp, 2)), dma((n_dp,)), dma((n_dp,)),
            dma((2, n_dp, 2)), dma((2, n_dp, 2)), dma((2,)), dma((2,)),
            dma((2, n_dp)), dma((2, n_dp)),
        ],
        compiler_params=pltpu.CompilerParams(
            collective_id=0, has_side_effects=True, vmem_limit_bytes=32 * 1024 * 1024
        ),
    )(*operands)
    return best.reshape(rows)


def general(embeddings, assignment, pair_list, capacity, n_dp, n_owner):
    rows, width = embeddings.shape
    slots = capacity * n_dp
    values = embeddings.astype(jnp.float32)
    unit = (values * lax.rsqrt(jnp.sum(values * values, axis=1, keepdims=True) + 1e-06)).astype(
        jnp.bfloat16
    )
    target = assignment // (n_owner * CPD)
    onehot = (target[:, None] == jnp.arange(n_dp, dtype=jnp.int32)[None, :]).astype(jnp.int32)
    slot = jnp.sum(jnp.cumsum(onehot, axis=0) * onehot, axis=1) - 1
    position = target * capacity + slot
    here_owner = lax.axis_index("owner")
    here_dp = lax.axis_index("dp")
    first_id = (here_dp * n_owner + here_owner) * CPD
    partners_mine = lax.dynamic_slice_in_dim(pair_list, first_id, CPD)
    start_best = jnp.full((slots,), -1.0, jnp.float32)
    send_rows = jnp.zeros((slots, width), jnp.bfloat16).at[position].set(unit)
    send_ids = jnp.full((slots,), -1, jnp.int32).at[position].set(assignment)
    got_rows, got_ids = (
        lax.all_to_all(
            send_rows.reshape(n_dp, capacity, width), "dp", split_axis=0, concat_axis=0, tiled=True
        ),
        lax.all_to_all(
            send_ids.reshape(n_dp, capacity), "dp", split_axis=0, concat_axis=0, tiled=True
        ),
    )
    mine = got_rows.reshape(slots, width)
    mine_ids = got_ids.reshape(slots)
    local = jnp.clip(mine_ids - first_id, 0, CPD - 1)
    picked = local[:, None] == jnp.arange(CPD, dtype=jnp.int32)[None, :]
    partner = jnp.sum(jnp.where(picked, partners_mine[None, :], 0), axis=1)
    rows_p = lax.all_gather(mine, "owner", axis=0, tiled=True)
    ids_p = lax.all_gather(mine_ids, "owner", axis=0, tiled=True)
    scores = lax.dot_general(mine, rows_p, NT, preferred_element_type=jnp.float32)
    column = jnp.arange(ids_p.shape[0], dtype=jnp.int32)
    itself = here_owner * slots + jnp.arange(slots, dtype=jnp.int32)
    same = (
        (mine_ids[:, None] == ids_p[None, :])
        & (ids_p[None, :] >= 0)
        & (itself[:, None] != column[None, :])
    )
    related = same | (partner[:, None] == ids_p[None, :])
    best = jnp.maximum(start_best, jnp.max(jnp.where(related, scores, -1.0), axis=1))
    returned = lax.all_to_all(
        best.reshape(n_dp, capacity), "dp", split_axis=0, concat_axis=0, tiled=True
    )
    return returned.reshape(slots)[position]


def shards(embeddings, assignment, pair_list):
    n_dp = lax.axis_size("dp")
    n_owner = lax.axis_size("owner")
    capacity = 2 * embeddings.shape[0] // n_dp
    whole_tiles = n_dp == 8 and n_owner == 4 and capacity % 16 == 0
    form = fused if whole_tiles else general
    return form(embeddings, assignment, pair_list, capacity, n_dp, n_owner)


def solution(mesh):
    placed = (P(("dp", "owner"), None), P(("dp", "owner")), P())
    return jax.shard_map(
        shards, mesh=mesh, in_specs=placed, out_specs=P(("dp", "owner")), check_vma=False
    )
```

```python
import functools

import jax
import jax.numpy as jnp
from jax import lax
from jax.experimental import pallas as pl
from jax.experimental.pallas import tpu as pltpu
from jax.sharding import PartitionSpec as P

CPD = 16
MESH = pl.DeviceIdType.MESH
NT = (((1,), (1,)), ((), ()))


def peer_of(d, k):
    z, y = d // 2, d % 2
    dz, dy = k // 2, k % 2
    if dz == 1:
        z = z + 1 - 2 * (z % 2)
    elif dz == 2:
        z = (z + 2) % 4
    elif dz == 3:
        z = 3 - z
    if dy:
        y = 1 - y
    return z * 2 + y


NEAR = (1, 2, 3)
CROSS = (4, 6, 5, 7)
PIECES = tuple((k, None) for k in CROSS)
AHEAD = 3
SEND_ORDER = (4, 6, 5, 7, 2, 3, 1)


def kernel(
    cap, n_dp, n_owner,
    emb_hbm, asg_hbm, pairs_hbm, out,
    emb, asg, pairs,
    send, own, sib, cpt,
    code_send, code_got, codes, columns, ret, res,
    in_s,
    row_ss, row_rs, id_ss, id_rs, fw_ss, fw_rs, cd_ss, cd_rs, rt_ss, rt_rs,
):
    rows, width = emb.shape
    slots = cap * n_dp
    loads = [
        pltpu.make_async_copy(src, dst, in_s.at[i])
        for i, (src, dst) in enumerate(((asg_hbm, asg), (emb_hbm, emb), (pairs_hbm, pairs)))
    ]
    for load in loads:
        load.start()
    d = lax.axis_index("dp")
    o = lax.axis_index("owner")
    o_sib = o + 1 - 2 * (o % 2)
    o_cpt = (o + 2) % 4
    peers = [peer_of(d, k) for k in range(n_dp)]

    barrier = pltpu.get_barrier_semaphore()
    for k in range(n_dp):
        if k:
            pl.semaphore_signal(barrier, inc=1, device_id=(peers[k], o), device_id_type=MESH)
        pl.semaphore_signal(barrier, inc=1, device_id=(peers[k], o_sib), device_id_type=MESH)
    for k in (0,) + NEAR:
        pl.semaphore_signal(barrier, inc=1, device_id=(peers[k], o_cpt), device_id_type=MESH)

    loads[0].wait()
    a = asg[...]
    t_row = lax.shift_right_logical(a, 6)
    code_row = ((a & 63) + 1).astype(jnp.float32)
    t_hot = (lax.broadcasted_iota(jnp.int32, (n_dp, rows), 0) == t_row).astype(jnp.float32)
    before = (
        lax.broadcasted_iota(jnp.int32, (rows, rows), 0)
        < lax.broadcasted_iota(jnp.int32, (rows, rows), 1)
    ).astype(jnp.float32).astype(jnp.bfloat16)
    count = jnp.dot(t_hot.astype(jnp.bfloat16), before, preferred_element_type=jnp.float32)
    rank = jnp.sum(t_hot * count, axis=0, keepdims=True).astype(jnp.int32)
    slot_iota = lax.broadcasted_iota(jnp.int32, (slots, rows), 0)
    loads[1].wait()
    values = emb[...].astype(jnp.float32)
    unit = (values * lax.rsqrt(jnp.sum(values * values, axis=1, keepdims=True) + 1e-06)).astype(
        jnp.bfloat16
    )
    position = t_row * cap + rank
    half = n_dp // 2
    near_base = (d // half) * half
    cross_base = half - near_base
    group_iota = lax.broadcasted_iota(jnp.int32, (half * cap, rows), 0)

    def pack(base):
        place = (group_iota + base * cap == position).astype(jnp.float32).astype(jnp.bfloat16)
        packed = jnp.dot(place, unit, preferred_element_type=jnp.float32).astype(jnp.bfloat16)
        send[pl.ds(base, half)] = packed.reshape(half, cap, width)

    pack(near_base)
    own[d] = send[d]

    pl.semaphore_wait(barrier, 2 * n_dp + len(NEAR))

    def part(h):
        return pl.ds(0, cap) if h is None else pl.ds(h * (cap // 2), cap // 2)

    def block_copy(k, h=None):
        p = peers[k]
        return pltpu.make_async_remote_copy(
            src_ref=send.at[p, part(h)], dst_ref=own.at[d, part(h)],
            send_sem=row_ss.at[k, h or 0], recv_sem=row_rs.at[k, h or 0],
            device_id=(p, o), device_id_type=MESH,
        )

    def code_copy(k):
        p = peers[k]
        return pltpu.make_async_remote_copy(
            src_ref=code_send.at[p], dst_ref=code_got.at[d], send_sem=id_ss.at[k],
            recv_sem=id_rs.at[k], device_id=(p, o), device_id_type=MESH,
        )

    def forward(k, which, h=None):
        s = peers[k]
        if which and k in NEAR:
            src, dst, target = send.at[s], cpt.at[d], (s, o_cpt)
        else:
            src, dst = own.at[s, part(h)], (sib, cpt)[which].at[s, part(h)]
            target = (d, (o_sib, o_cpt)[which])
        return pltpu.make_async_remote_copy(
            src_ref=src, dst_ref=dst,
            send_sem=fw_ss.at[which, k, h or 0], recv_sem=fw_rs.at[which, k, h or 0],
            device_id=target, device_id_type=MESH,
        )

    def codes_copy(which):
        return pltpu.make_async_remote_copy(
            src_ref=codes.at[0], dst_ref=codes.at[1 + which], send_sem=cd_ss.at[which],
            recv_sem=cd_rs.at[which], device_id=(d, (o_sib, o_cpt)[which]), device_id_type=MESH,
        )

    def back(k, which):
        s = peers[k]
        return pltpu.make_async_remote_copy(
            src_ref=res.at[which], dst_ref=ret.at[which, d], send_sem=rt_ss.at[which, k],
            recv_sem=rt_rs.at[which, k], device_id=(s, (o, o_sib)[which]), device_id_type=MESH,
        )

    for k in NEAR:
        block_copy(k).start()
    forward(0, 1).start()
    for k in NEAR:
        forward(k, 1).start()
    pack(cross_base)
    for k, h in PIECES[:2]:
        block_copy(k, h).start()
    lane_hot = (slot_iota == d * cap + rank).astype(jnp.float32)
    slot_codes = lax.dot_general(
        (t_hot * code_row).astype(jnp.bfloat16),
        lane_hot.astype(jnp.bfloat16),
        NT,
        preferred_element_type=jnp.float32,
    )
    for t in range(n_dp):
        code_send[t] = slot_codes[t : t + 1, :]
    code_got[d] = code_send[d]
    for k in SEND_ORDER:
        code_copy(k).start()
    forward(0, 0).start()
    for k in NEAR:
        block_copy(k).wait_recv()
        forward(k, 0).start()
        if k == 2:
            block_copy(*PIECES[2]).start()
    for k in NEAR + CROSS:
        code_copy(k).wait_recv()
    codes[0] = jnp.sum(code_got[...], axis=0)
    codes_copy(0).start()
    codes_copy(1).start()
    loads[2].wait()
    g_own = codes[0]

    def pieces(first, last):
        for i in range(first, last):
            k, h = PIECES[i]
            block_copy(k, h).wait_recv()
            forward(k, 1, h).start()
            if h != 0:
                forward(k, 0).start()
            if i + AHEAD < len(PIECES):
                block_copy(*PIECES[i + AHEAD]).start()

    def partner(g, owner):
        found = jnp.full(g.shape, -1, jnp.int32)
        for c in range(CPD):
            other = pairs[(d * n_owner + owner) * CPD + c] - d * (n_owner * CPD) + 1
            found = jnp.where(g == (owner * CPD + c + 1).astype(jnp.float32), other, found)
        return found.astype(jnp.float32)

    def column(g):
        return jnp.transpose(jnp.broadcast_to(g, (128, slots)))

    p_own = partner(g_own, o)
    columns[0] = column(g_own)
    pieces(0, 1)
    codes_copy(0).wait_recv()
    codes_copy(1).wait_recv()
    p_sib = partner(codes[1], o_sib)
    columns[1] = column(codes[1])
    columns[2] = column(codes[2])
    pieces(1, len(PIECES))

    def table(ref):
        return ref[...].reshape(slots, width)

    def scores(keys, queries):
        return lax.dot_general(keys, queries, NT, preferred_element_type=jnp.float32)

    def wide(column_128):
        return jnp.concatenate([column_128] * (slots // 128), axis=1)

    def masked_max(s, mask):
        return jnp.max(jnp.where(mask, s, -1.0), axis=0, keepdims=True)

    rows_own = table(own)
    key = lax.broadcasted_iota(jnp.int32, (slots, slots), 0)
    query = lax.broadcasted_iota(jnp.int32, (slots, slots), 1)
    best = masked_max(scores(rows_own, rows_own), (wide(columns[0]) == g_own) & (key != query))
    for k in range(n_dp):
        forward(k, 0).wait_recv()
    rows_sib = table(sib)
    best = jnp.maximum(best, masked_max(scores(rows_sib, rows_own), wide(columns[1]) == p_own))
    best_sib = jnp.full((1, slots), -1.0, jnp.float32)

    def neighbour_keys(base):
        keys = cpt[pl.ds(base, half)].reshape(half * cap, width)
        return keys, wide(columns[2, pl.ds(pl.multiple_of(base * cap, half * cap), half * cap)])

    for k in (0,) + NEAR:
        forward(k, 1).wait_recv()
    keys, key_codes = neighbour_keys(near_base)
    best_sib = jnp.maximum(best_sib, masked_max(scores(keys, rows_sib), key_codes == p_sib))
    best = jnp.maximum(best, masked_max(scores(keys, rows_own), key_codes == p_own))
    for k, h in PIECES:
        forward(k, 1, h).wait_recv()
    keys, key_codes = neighbour_keys(cross_base)
    res[1] = jnp.maximum(best_sib, masked_max(scores(keys, rows_sib), key_codes == p_sib))
    for k in (4, 5, 6, 7, 2, 3, 1, 0):
        back(k, 1).start()
    best = jnp.maximum(best, masked_max(scores(keys, rows_own), key_codes == p_own))
    res[0] = best
    for k in SEND_ORDER:
        back(k, 0).start()
    ret[0, d] = best

    for k in range(n_dp):
        back(k, 1).wait_recv()
        if k:
            back(k, 0).wait_recv()
    got = jnp.concatenate([jnp.maximum(ret[0, t], ret[1, t]) for t in range(n_dp)], axis=0)
    picked = lax.dot_general(
        got, lane_hot, (((1,), (0,)), ((), ())),
        preferred_element_type=jnp.float32, precision=lax.Precision.HIGHEST,
    )
    out[...] = jnp.maximum(jnp.sum(t_hot * picked, axis=0, keepdims=True), -1.0)

    for k in (0,) + NEAR + CROSS:
        if k:
            code_copy(k).wait_send()
            back(k, 0).wait_send()
        if k in NEAR:
            block_copy(k).wait_send()
        if k not in CROSS:
            forward(k, 1).wait_send()
        back(k, 1).wait_send()
        forward(k, 0).wait_send()
    for k, h in PIECES:
        block_copy(k, h).wait_send()
        forward(k, 1, h).wait_send()
    codes_copy(0).wait_send()
    codes_copy(1).wait_send()


def fused(embeddings, assignment, pair_list, capacity, n_dp, n_owner):
    rows, width = embeddings.shape
    slots = capacity * n_dp
    block = pltpu.VMEM((n_dp, capacity, width), jnp.bfloat16)
    line = pltpu.VMEM((n_dp, 1, slots), jnp.float32)
    dma = pltpu.SemaphoreType.DMA
    operands = [
        pltpu.with_memory_space_constraint(x, pltpu.HBM)
        for x in (embeddings, assignment.reshape(1, rows), pair_list)
    ]
    best = pl.pallas_call(
        functools.partial(kernel, capacity, n_dp, n_owner),
        out_shape=jax.ShapeDtypeStruct((1, rows), jnp.float32),
        in_specs=[pl.BlockSpec(memory_space=pl.ANY)] * 3,
        out_specs=pl.BlockSpec(memory_space=pltpu.VMEM),
        scratch_shapes=[
            pltpu.VMEM((rows, width), jnp.bfloat16),
            pltpu.VMEM((1, rows), jnp.int32),
            pltpu.SMEM(pair_list.shape, jnp.int32),
            block, block, block, block,
            line, line,
            pltpu.VMEM((3, 1, slots), jnp.float32),
            pltpu.VMEM((3, slots, 128), jnp.float32),
            pltpu.VMEM((2, n_dp, 1, slots), jnp.float32),
            pltpu.VMEM((2, 1, slots), jnp.float32),
            dma((3,)),
            dma((n_dp, 2)), dma((n_dp, 2)), dma((n_dp,)), dma((n_dp,)),
            dma((2, n_dp, 2)), dma((2, n_dp, 2)), dma((2,)), dma((2,)),
            dma((2, n_dp)), dma((2, n_dp)),
        ],
        compiler_params=pltpu.CompilerParams(
            collective_id=0, has_side_effects=True, vmem_limit_bytes=32 * 1024 * 1024
        ),
    )(*operands)
    return best.reshape(rows)


def general(embeddings, assignment, pair_list, capacity, n_dp, n_owner):
    rows, width = embeddings.shape
    slots = capacity * n_dp
    values = embeddings.astype(jnp.float32)
    unit = (values * lax.rsqrt(jnp.sum(values * values, axis=1, keepdims=True) + 1e-06)).astype(
        jnp.bfloat16
    )
    target = assignment // (n_owner * CPD)
    onehot = (target[:, None] == jnp.arange(n_dp, dtype=jnp.int32)[None, :]).astype(jnp.int32)
    slot = jnp.sum(jnp.cumsum(onehot, axis=0) * onehot, axis=1) - 1
    position = target * capacity + slot
    here_owner = lax.axis_index("owner")
    here_dp = lax.axis_index("dp")
    first_id = (here_dp * n_owner + here_owner) * CPD
    partners_mine = lax.dynamic_slice_in_dim(pair_list, first_id, CPD)
    start_best = jnp.full((slots,), -1.0, jnp.float32)
    send_rows = jnp.zeros((slots, width), jnp.bfloat16).at[position].set(unit)
    send_ids = jnp.full((slots,), -1, jnp.int32).at[position].set(assignment)
    got_rows, got_ids = (
        lax.all_to_all(
            send_rows.reshape(n_dp, capacity, width), "dp", split_axis=0, concat_axis=0, tiled=True
        ),
        lax.all_to_all(
            send_ids.reshape(n_dp, capacity), "dp", split_axis=0, concat_axis=0, tiled=True
        ),
    )
    mine = got_rows.reshape(slots, width)
    mine_ids = got_ids.reshape(slots)
    local = jnp.clip(mine_ids - first_id, 0, CPD - 1)
    picked = local[:, None] == jnp.arange(CPD, dtype=jnp.int32)[None, :]
    partner = jnp.sum(jnp.where(picked, partners_mine[None, :], 0), axis=1)
    rows_p = lax.all_gather(mine, "owner", axis=0, tiled=True)
    ids_p = lax.all_gather(mine_ids, "owner", axis=0, tiled=True)
    scores = lax.dot_general(mine, rows_p, NT, preferred_element_type=jnp.float32)
    column = jnp.arange(ids_p.shape[0], dtype=jnp.int32)
    itself = here_owner * slots + jnp.arange(slots, dtype=jnp.int32)
    same = (
        (mine_ids[:, None] == ids_p[None, :])
        & (ids_p[None, :] >= 0)
        & (itself[:, None] != column[None, :])
    )
    related = same | (partner[:, None] == ids_p[None, :])
    best = jnp.maximum(start_best, jnp.max(jnp.where(related, scores, -1.0), axis=1))
    returned = lax.all_to_all(
        best.reshape(n_dp, capacity), "dp", split_axis=0, concat_axis=0, tiled=True
    )
    return returned.reshape(slots)[position]


def shards(embeddings, assignment, pair_list):
    n_dp = lax.axis_size("dp")
    n_owner = lax.axis_size("owner")
    capacity = 2 * embeddings.shape[0] // n_dp
    whole_tiles = n_dp == 8 and n_owner == 4 and capacity % 16 == 0
    form = fused if whole_tiles else general
    return form(embeddings, assignment, pair_list, capacity, n_dp, n_owner)


def solution(mesh):
    placed = (P(("dp", "owner"), None), P(("dp", "owner")), P())
    return jax.shard_map(
        shards, mesh=mesh, in_specs=placed, out_specs=P(("dp", "owner")), check_vma=False
    )
```

```python
import functools

import jax
import jax.numpy as jnp
from jax import lax
from jax.experimental import pallas as pl
from jax.experimental.pallas import tpu as pltpu
from jax.sharding import PartitionSpec as P

CPD = 16
MESH = pl.DeviceIdType.MESH
NT = (((1,), (1,)), ((), ()))


def peer_of(d, k):
    z, y = d // 2, d % 2
    dz, dy = k // 2, k % 2
    if dz == 1:
        z = z + 1 - 2 * (z % 2)
    elif dz == 2:
        z = (z + 2) % 4
    elif dz == 3:
        z = 3 - z
    if dy:
        y = 1 - y
    return z * 2 + y


NEAR = (1, 2, 3)
CROSS = (4, 6, 5, 7)
PIECES = tuple((k, None) for k in CROSS)
AHEAD = 3
SEND_ORDER = (4, 6, 5, 7, 2, 3, 1)


def kernel(
    cap, n_dp, n_owner,
    emb_hbm, asg_hbm, pairs_hbm, out,
    emb, asg, pairs,
    send, own, sib, cpt,
    code_send, code_got, codes, columns, ret, res,
    in_s,
    row_ss, row_rs, id_ss, id_rs, fw_ss, fw_rs, cd_ss, cd_rs, rt_ss, rt_rs,
):
    rows, width = emb.shape
    slots = cap * n_dp
    loads = [
        pltpu.make_async_copy(src, dst, in_s.at[i])
        for i, (src, dst) in enumerate(((asg_hbm, asg), (emb_hbm, emb), (pairs_hbm, pairs)))
    ]
    for load in loads:
        load.start()
    d = lax.axis_index("dp")
    o = lax.axis_index("owner")
    o_sib = o + 1 - 2 * (o % 2)
    o_cpt = (o + 2) % 4
    peers = [peer_of(d, k) for k in range(n_dp)]

    barrier = pltpu.get_barrier_semaphore()
    for k in range(n_dp):
        if k:
            pl.semaphore_signal(barrier, inc=1, device_id=(peers[k], o), device_id_type=MESH)
        pl.semaphore_signal(barrier, inc=1, device_id=(peers[k], o_sib), device_id_type=MESH)
    pl.semaphore_signal(barrier, inc=1, device_id=(d, o_cpt), device_id_type=MESH)

    loads[0].wait()
    a = asg[...]
    t_row = lax.shift_right_logical(a, 6)
    code_row = ((a & 63) + 1).astype(jnp.float32)
    t_hot = (lax.broadcasted_iota(jnp.int32, (n_dp, rows), 0) == t_row).astype(jnp.float32)
    before = (
        lax.broadcasted_iota(jnp.int32, (rows, rows), 0)
        < lax.broadcasted_iota(jnp.int32, (rows, rows), 1)
    ).astype(jnp.float32).astype(jnp.bfloat16)
    count = jnp.dot(t_hot.astype(jnp.bfloat16), before, preferred_element_type=jnp.float32)
    rank = jnp.sum(t_hot * count, axis=0, keepdims=True).astype(jnp.int32)
    slot_iota = lax.broadcasted_iota(jnp.int32, (slots, rows), 0)
    loads[1].wait()
    values = emb[...].astype(jnp.float32)
    unit = (values * lax.rsqrt(jnp.sum(values * values, axis=1, keepdims=True) + 1e-06)).astype(
        jnp.bfloat16
    )
    position = t_row * cap + rank
    half = n_dp // 2
    near_base = (d // half) * half
    cross_base = half - near_base
    group_iota = lax.broadcasted_iota(jnp.int32, (half * cap, rows), 0)

    def pack(base):
        place = (group_iota + base * cap == position).astype(jnp.float32).astype(jnp.bfloat16)
        packed = jnp.dot(place, unit, preferred_element_type=jnp.float32).astype(jnp.bfloat16)
        send[pl.ds(base, half)] = packed.reshape(half, cap, width)

    pack(near_base)
    own[d] = send[d]

    pl.semaphore_wait(barrier, 2 * n_dp)

    def part(h):
        return pl.ds(0, cap) if h is None else pl.ds(h * (cap // 2), cap // 2)

    def block_copy(k, h=None):
        p = peers[k]
        return pltpu.make_async_remote_copy(
            src_ref=send.at[p, part(h)], dst_ref=own.at[d, part(h)],
            send_sem=row_ss.at[k, h or 0], recv_sem=row_rs.at[k, h or 0],
            device_id=(p, o), device_id_type=MESH,
        )

    def code_copy(k):
        p = peers[k]
        return pltpu.make_async_remote_copy(
            src_ref=code_send.at[p], dst_ref=code_got.at[d], send_sem=id_ss.at[k],
            recv_sem=id_rs.at[k], device_id=(p, o), device_id_type=MESH,
        )

    def forward(k, which, h=None):
        s = peers[k]
        return pltpu.make_async_remote_copy(
            src_ref=own.at[s, part(h)], dst_ref=(sib, cpt)[which].at[s, part(h)],
            send_sem=fw_ss.at[which, k, h or 0], recv_sem=fw_rs.at[which, k, h or 0],
            device_id=(d, (o_sib, o_cpt)[which]), device_id_type=MESH,
        )

    def codes_copy(which):
        return pltpu.make_async_remote_copy(
            src_ref=codes.at[0], dst_ref=codes.at[1 + which], send_sem=cd_ss.at[which],
            recv_sem=cd_rs.at[which], device_id=(d, (o_sib, o_cpt)[which]), device_id_type=MESH,
        )

    def back(k, which):
        s = peers[k]
        return pltpu.make_async_remote_copy(
            src_ref=res.at[which], dst_ref=ret.at[which, d], send_sem=rt_ss.at[which, k],
            recv_sem=rt_rs.at[which, k], device_id=(s, (o, o_sib)[which]), device_id_type=MESH,
        )

    for k in NEAR:
        block_copy(k).start()
    forward(0, 1).start()
    pack(cross_base)
    for k, h in PIECES[:2]:
        block_copy(k, h).start()
    lane_hot = (slot_iota == d * cap + rank).astype(jnp.float32)
    slot_codes = lax.dot_general(
        (t_hot * code_row).astype(jnp.bfloat16),
        lane_hot.astype(jnp.bfloat16),
        NT,
        preferred_element_type=jnp.float32,
    )
    for t in range(n_dp):
        code_send[t] = slot_codes[t : t + 1, :]
    code_got[d] = code_send[d]
    for k in SEND_ORDER:
        code_copy(k).start()
    for k in NEAR:
        block_copy(k).wait_recv()
        forward(k, 1).start()
        if k == 2:
            block_copy(*PIECES[2]).start()
    for k in (0,) + NEAR:
        forward(k, 0).start()
    for k in NEAR + CROSS:
        code_copy(k).wait_recv()
    codes[0] = jnp.sum(code_got[...], axis=0)
    codes_copy(0).start()
    codes_copy(1).start()
    loads[2].wait()
    g_own = codes[0]

    def pieces(first, last):
        for i in range(first, last):
            k, h = PIECES[i]
            block_copy(k, h).wait_recv()
            forward(k, 1, h).start()
            if h != 0:
                forward(k, 0).start()
            if i + AHEAD < len(PIECES):
                block_copy(*PIECES[i + AHEAD]).start()

    def partner(g, owner):
        found = jnp.full(g.shape, -1, jnp.int32)
        for c in range(CPD):
            other = pairs[(d * n_owner + owner) * CPD + c] - d * (n_owner * CPD) + 1
            found = jnp.where(g == (owner * CPD + c + 1).astype(jnp.float32), other, found)
        return found.astype(jnp.float32)

    def column(g):
        return jnp.transpose(jnp.broadcast_to(g, (128, slots)))

    p_own = partner(g_own, o)
    columns[0] = column(g_own)
    pieces(0, 1)
    codes_copy(0).wait_recv()
    codes_copy(1).wait_recv()
    p_sib = partner(codes[1], o_sib)
    columns[1] = column(codes[1])
    columns[2] = column(codes[2])
    pieces(1, len(PIECES))

    def table(ref):
        return ref[...].reshape(slots, width)

    def scores(keys, queries):
        return lax.dot_general(keys, queries, NT, preferred_element_type=jnp.float32)

    def wide(column_128):
        return jnp.concatenate([column_128] * (slots // 128), axis=1)

    def masked_max(s, mask):
        return jnp.max(jnp.where(mask, s, -1.0), axis=0, keepdims=True)

    rows_own = table(own)
    key = lax.broadcasted_iota(jnp.int32, (slots, slots), 0)
    query = lax.broadcasted_iota(jnp.int32, (slots, slots), 1)
    best = masked_max(scores(rows_own, rows_own), (wide(columns[0]) == g_own) & (key != query))
    for k in range(n_dp):
        forward(k, 0).wait_recv()
    rows_sib = table(sib)
    best = jnp.maximum(best, masked_max(scores(rows_sib, rows_own), wide(columns[1]) == p_own))
    best_sib = jnp.full((1, slots), -1.0, jnp.float32)

    def neighbour_keys(base):
        keys = cpt[pl.ds(base, half)].reshape(half * cap, width)
        return keys, wide(columns[2, pl.ds(pl.multiple_of(base * cap, half * cap), half * cap)])

    for k in (0,) + NEAR:
        forward(k, 1).wait_recv()
    keys, key_codes = neighbour_keys(near_base)
    best_sib = jnp.maximum(best_sib, masked_max(scores(keys, rows_sib), key_codes == p_sib))
    best = jnp.maximum(best, masked_max(scores(keys, rows_own), key_codes == p_own))
    for k, h in PIECES:
        forward(k, 1, h).wait_recv()
    keys, key_codes = neighbour_keys(cross_base)
    res[1] = jnp.maximum(best_sib, masked_max(scores(keys, rows_sib), key_codes == p_sib))
    for k in (4, 5, 6, 7, 2, 3, 1, 0):
        back(k, 1).start()
    best = jnp.maximum(best, masked_max(scores(keys, rows_own), key_codes == p_own))
    res[0] = best
    for k in SEND_ORDER:
        back(k, 0).start()
    ret[0, d] = best

    for k in range(n_dp):
        back(k, 1).wait_recv()
        if k:
            back(k, 0).wait_recv()
    got = jnp.concatenate([jnp.maximum(ret[0, t], ret[1, t]) for t in range(n_dp)], axis=0)
    picked = lax.dot_general(
        got, lane_hot, (((1,), (0,)), ((), ())),
        preferred_element_type=jnp.float32, precision=lax.Precision.HIGHEST,
    )
    out[...] = jnp.maximum(jnp.sum(t_hot * picked, axis=0, keepdims=True), -1.0)

    for k in (0,) + NEAR + CROSS:
        if k:
            code_copy(k).wait_send()
            back(k, 0).wait_send()
        if k in NEAR:
            block_copy(k).wait_send()
        if k not in CROSS:
            forward(k, 1).wait_send()
        back(k, 1).wait_send()
        forward(k, 0).wait_send()
    for k, h in PIECES:
        block_copy(k, h).wait_send()
        forward(k, 1, h).wait_send()
    codes_copy(0).wait_send()
    codes_copy(1).wait_send()


def fused(embeddings, assignment, pair_list, capacity, n_dp, n_owner):
    rows, width = embeddings.shape
    slots = capacity * n_dp
    block = pltpu.VMEM((n_dp, capacity, width), jnp.bfloat16)
    line = pltpu.VMEM((n_dp, 1, slots), jnp.float32)
    dma = pltpu.SemaphoreType.DMA
    operands = [
        pltpu.with_memory_space_constraint(x, pltpu.HBM)
        for x in (embeddings, assignment.reshape(1, rows), pair_list)
    ]
    best = pl.pallas_call(
        functools.partial(kernel, capacity, n_dp, n_owner),
        out_shape=jax.ShapeDtypeStruct((1, rows), jnp.float32),
        in_specs=[pl.BlockSpec(memory_space=pl.ANY)] * 3,
        out_specs=pl.BlockSpec(memory_space=pltpu.VMEM),
        scratch_shapes=[
            pltpu.VMEM((rows, width), jnp.bfloat16),
            pltpu.VMEM((1, rows), jnp.int32),
            pltpu.SMEM(pair_list.shape, jnp.int32),
            block, block, block, block,
            line, line,
            pltpu.VMEM((3, 1, slots), jnp.float32),
            pltpu.VMEM((3, slots, 128), jnp.float32),
            pltpu.VMEM((2, n_dp, 1, slots), jnp.float32),
            pltpu.VMEM((2, 1, slots), jnp.float32),
            dma((3,)),
            dma((n_dp, 2)), dma((n_dp, 2)), dma((n_dp,)), dma((n_dp,)),
            dma((2, n_dp, 2)), dma((2, n_dp, 2)), dma((2,)), dma((2,)),
            dma((2, n_dp)), dma((2, n_dp)),
        ],
        compiler_params=pltpu.CompilerParams(
            collective_id=0, has_side_effects=True, vmem_limit_bytes=32 * 1024 * 1024
        ),
    )(*operands)
    return best.reshape(rows)


def general(embeddings, assignment, pair_list, capacity, n_dp, n_owner):
    rows, width = embeddings.shape
    slots = capacity * n_dp
    values = embeddings.astype(jnp.float32)
    unit = (values * lax.rsqrt(jnp.sum(values * values, axis=1, keepdims=True) + 1e-06)).astype(
        jnp.bfloat16
    )
    target = assignment // (n_owner * CPD)
    onehot = (target[:, None] == jnp.arange(n_dp, dtype=jnp.int32)[None, :]).astype(jnp.int32)
    slot = jnp.sum(jnp.cumsum(onehot, axis=0) * onehot, axis=1) - 1
    position = target * capacity + slot
    here_owner = lax.axis_index("owner")
    here_dp = lax.axis_index("dp")
    first_id = (here_dp * n_owner + here_owner) * CPD
    partners_mine = lax.dynamic_slice_in_dim(pair_list, first_id, CPD)
    start_best = jnp.full((slots,), -1.0, jnp.float32)
    send_rows = jnp.zeros((slots, width), jnp.bfloat16).at[position].set(unit)
    send_ids = jnp.full((slots,), -1, jnp.int32).at[position].set(assignment)
    got_rows, got_ids = (
        lax.all_to_all(
            send_rows.reshape(n_dp, capacity, width), "dp", split_axis=0, concat_axis=0, tiled=True
        ),
        lax.all_to_all(
            send_ids.reshape(n_dp, capacity), "dp", split_axis=0, concat_axis=0, tiled=True
        ),
    )
    mine = got_rows.reshape(slots, width)
    mine_ids = got_ids.reshape(slots)
    local = jnp.clip(mine_ids - first_id, 0, CPD - 1)
    picked = local[:, None] == jnp.arange(CPD, dtype=jnp.int32)[None, :]
    partner = jnp.sum(jnp.where(picked, partners_mine[None, :], 0), axis=1)
    rows_p = lax.all_gather(mine, "owner", axis=0, tiled=True)
    ids_p = lax.all_gather(mine_ids, "owner", axis=0, tiled=True)
    scores = lax.dot_general(mine, rows_p, NT, preferred_element_type=jnp.float32)
    column = jnp.arange(ids_p.shape[0], dtype=jnp.int32)
    itself = here_owner * slots + jnp.arange(slots, dtype=jnp.int32)
    same = (
        (mine_ids[:, None] == ids_p[None, :])
        & (ids_p[None, :] >= 0)
        & (itself[:, None] != column[None, :])
    )
    related = same | (partner[:, None] == ids_p[None, :])
    best = jnp.maximum(start_best, jnp.max(jnp.where(related, scores, -1.0), axis=1))
    returned = lax.all_to_all(
        best.reshape(n_dp, capacity), "dp", split_axis=0, concat_axis=0, tiled=True
    )
    return returned.reshape(slots)[position]


def shards(embeddings, assignment, pair_list):
    n_dp = lax.axis_size("dp")
    n_owner = lax.axis_size("owner")
    capacity = 2 * embeddings.shape[0] // n_dp
    whole_tiles = n_dp == 8 and n_owner == 4 and capacity % 16 == 0
    form = fused if whole_tiles else general
    return form(embeddings, assignment, pair_list, capacity, n_dp, n_owner)


def solution(mesh):
    placed = (P(("dp", "owner"), None), P(("dp", "owner")), P())
    return jax.shard_map(
        shards, mesh=mesh, in_specs=placed, out_specs=P(("dp", "owner")), check_vma=False
    )
```

```python
import functools

import jax
import jax.numpy as jnp
from jax import lax
from jax.experimental import pallas as pl
from jax.experimental.pallas import tpu as pltpu
from jax.sharding import PartitionSpec as P

CPD = 16
MESH = pl.DeviceIdType.MESH
NT = (((1,), (1,)), ((), ()))


def peer_of(d, k):
    z, y = d // 2, d % 2
    dz, dy = k // 2, k % 2
    if dz == 1:
        z = z + 1 - 2 * (z % 2)
    elif dz == 2:
        z = (z + 2) % 4
    elif dz == 3:
        z = 3 - z
    if dy:
        y = 1 - y
    return z * 2 + y


NEAR = (1, 2, 3)
CROSS = (4, 6, 5, 7)
PIECES = tuple((k, None) for k in CROSS)
AHEAD = 3
SEND_ORDER = (4, 6, 5, 7, 2, 3, 1)


def kernel(
    cap, n_dp, n_owner,
    emb_hbm, asg_hbm, pairs_hbm, out,
    emb, asg, pairs,
    send, own, sib, cpt,
    code_send, code_got, codes, columns, ret, res,
    in_s,
    row_ss, row_rs, id_ss, id_rs, fw_ss, fw_rs, cd_ss, cd_rs, rt_ss, rt_rs,
):
    rows, width = emb.shape
    slots = cap * n_dp
    loads = [
        pltpu.make_async_copy(src, dst, in_s.at[i])
        for i, (src, dst) in enumerate(((asg_hbm, asg), (emb_hbm, emb), (pairs_hbm, pairs)))
    ]
    for load in loads:
        load.start()
    d = lax.axis_index("dp")
    o = lax.axis_index("owner")
    o_sib = o + 1 - 2 * (o % 2)
    o_cpt = (o + 2) % 4
    peers = [peer_of(d, k) for k in range(n_dp)]

    barrier = pltpu.get_barrier_semaphore()
    for k in range(n_dp):
        if k:
            pl.semaphore_signal(barrier, inc=1, device_id=(peers[k], o), device_id_type=MESH)
        pl.semaphore_signal(barrier, inc=1, device_id=(peers[k], o_sib), device_id_type=MESH)
    pl.semaphore_signal(barrier, inc=1, device_id=(d, o_cpt), device_id_type=MESH)

    loads[0].wait()
    a = asg[...]
    t_row = lax.shift_right_logical(a, 6)
    code_row = ((a & 63) + 1).astype(jnp.float32)
    t_hot = (lax.broadcasted_iota(jnp.int32, (n_dp, rows), 0) == t_row).astype(jnp.float32)
    before = (
        lax.broadcasted_iota(jnp.int32, (rows, rows), 0)
        < lax.broadcasted_iota(jnp.int32, (rows, rows), 1)
    ).astype(jnp.float32).astype(jnp.bfloat16)
    count = jnp.dot(t_hot.astype(jnp.bfloat16), before, preferred_element_type=jnp.float32)
    rank = jnp.sum(t_hot * count, axis=0, keepdims=True).astype(jnp.int32)
    slot_iota = lax.broadcasted_iota(jnp.int32, (slots, rows), 0)
    lane_hot = (slot_iota == d * cap + rank).astype(jnp.float32)
    slot_codes = lax.dot_general(
        (t_hot * code_row).astype(jnp.bfloat16),
        lane_hot.astype(jnp.bfloat16),
        NT,
        preferred_element_type=jnp.float32,
    )
    for t in range(n_dp):
        code_send[t] = slot_codes[t : t + 1, :]

    loads[1].wait()
    values = emb[...].astype(jnp.float32)
    unit = (values * lax.rsqrt(jnp.sum(values * values, axis=1, keepdims=True) + 1e-06)).astype(
        jnp.bfloat16
    )
    position = t_row * cap + rank
    half = n_dp // 2
    near_base = (d // half) * half
    cross_base = half - near_base
    group_iota = lax.broadcasted_iota(jnp.int32, (half * cap, rows), 0)

    def pack(base):
        place = (group_iota + base * cap == position).astype(jnp.float32).astype(jnp.bfloat16)
        packed = jnp.dot(place, unit, preferred_element_type=jnp.float32).astype(jnp.bfloat16)
        send[pl.ds(base, half)] = packed.reshape(half, cap, width)

    pack(near_base)
    own[d] = send[d]
    code_got[d] = code_send[d]

    pl.semaphore_wait(barrier, 2 * n_dp)

    def part(h):
        return pl.ds(0, cap) if h is None else pl.ds(h * (cap // 2), cap // 2)

    def block_copy(k, h=None):
        p = peers[k]
        return pltpu.make_async_remote_copy(
            src_ref=send.at[p, part(h)], dst_ref=own.at[d, part(h)],
            send_sem=row_ss.at[k, h or 0], recv_sem=row_rs.at[k, h or 0],
            device_id=(p, o), device_id_type=MESH,
        )

    def code_copy(k):
        p = peers[k]
        return pltpu.make_async_remote_copy(
            src_ref=code_send.at[p], dst_ref=code_got.at[d], send_sem=id_ss.at[k],
            recv_sem=id_rs.at[k], device_id=(p, o), device_id_type=MESH,
        )

    def forward(k, which, h=None):
        s = peers[k]
        return pltpu.make_async_remote_copy(
            src_ref=own.at[s, part(h)], dst_ref=(sib, cpt)[which].at[s, part(h)],
            send_sem=fw_ss.at[which, k, h or 0], recv_sem=fw_rs.at[which, k, h or 0],
            device_id=(d, (o_sib, o_cpt)[which]), device_id_type=MESH,
        )

    def codes_copy(which):
        return pltpu.make_async_remote_copy(
            src_ref=codes.at[0], dst_ref=codes.at[1 + which], send_sem=cd_ss.at[which],
            recv_sem=cd_rs.at[which], device_id=(d, (o_sib, o_cpt)[which]), device_id_type=MESH,
        )

    def back(k, which):
        s = peers[k]
        return pltpu.make_async_remote_copy(
            src_ref=res.at[which], dst_ref=ret.at[which, d], send_sem=rt_ss.at[which, k],
            recv_sem=rt_rs.at[which, k], device_id=(s, (o, o_sib)[which]), device_id_type=MESH,
        )

    for k in NEAR:
        block_copy(k).start()
    forward(0, 1).start()
    for k in SEND_ORDER:
        code_copy(k).start()
    pack(cross_base)
    for k, h in PIECES[:1]:
        block_copy(k, h).start()
    for k in NEAR:
        block_copy(k).wait_recv()
        forward(k, 1).start()
        if k != 2:
            block_copy(*PIECES[(k + 1) // 2]).start()
    for k in (0,) + NEAR:
        forward(k, 0).start()
    for k in NEAR + CROSS:
        code_copy(k).wait_recv()
    codes[0] = jnp.sum(code_got[...], axis=0)
    codes_copy(0).start()
    codes_copy(1).start()
    loads[2].wait()
    g_own = codes[0]

    def pieces(first, last):
        for i in range(first, last):
            k, h = PIECES[i]
            block_copy(k, h).wait_recv()
            forward(k, 1, h).start()
            if h != 0:
                forward(k, 0).start()
            if i + AHEAD < len(PIECES):
                block_copy(*PIECES[i + AHEAD]).start()

    def partner(g, owner):
        found = jnp.full(g.shape, -1, jnp.int32)
        for c in range(CPD):
            other = pairs[(d * n_owner + owner) * CPD + c] - d * (n_owner * CPD) + 1
            found = jnp.where(g == (owner * CPD + c + 1).astype(jnp.float32), other, found)
        return found.astype(jnp.float32)

    def column(g):
        return jnp.transpose(jnp.broadcast_to(g, (128, slots)))

    p_own = partner(g_own, o)
    columns[0] = column(g_own)
    pieces(0, 1)
    codes_copy(0).wait_recv()
    codes_copy(1).wait_recv()
    p_sib = partner(codes[1], o_sib)
    columns[1] = column(codes[1])
    columns[2] = column(codes[2])
    pieces(1, len(PIECES))

    def table(ref):
        return ref[...].reshape(slots, width)

    def scores(keys, queries):
        return lax.dot_general(keys, queries, NT, preferred_element_type=jnp.float32)

    def wide(column_128):
        return jnp.concatenate([column_128] * (slots // 128), axis=1)

    def masked_max(s, mask):
        return jnp.max(jnp.where(mask, s, -1.0), axis=0, keepdims=True)

    rows_own = table(own)
    key = lax.broadcasted_iota(jnp.int32, (slots, slots), 0)
    query = lax.broadcasted_iota(jnp.int32, (slots, slots), 1)
    best = masked_max(scores(rows_own, rows_own), (wide(columns[0]) == g_own) & (key != query))
    for k in range(n_dp):
        forward(k, 0).wait_recv()
    rows_sib = table(sib)
    best = jnp.maximum(best, masked_max(scores(rows_sib, rows_own), wide(columns[1]) == p_own))
    best_sib = jnp.full((1, slots), -1.0, jnp.float32)

    def neighbour_keys(base):
        keys = cpt[pl.ds(base, half)].reshape(half * cap, width)
        return keys, wide(columns[2, pl.ds(pl.multiple_of(base * cap, half * cap), half * cap)])

    for k in (0,) + NEAR:
        forward(k, 1).wait_recv()
    keys, key_codes = neighbour_keys(near_base)
    best_sib = jnp.maximum(best_sib, masked_max(scores(keys, rows_sib), key_codes == p_sib))
    best = jnp.maximum(best, masked_max(scores(keys, rows_own), key_codes == p_own))
    for k, h in PIECES:
        forward(k, 1, h).wait_recv()
    keys, key_codes = neighbour_keys(cross_base)
    res[1] = jnp.maximum(best_sib, masked_max(scores(keys, rows_sib), key_codes == p_sib))
    for k in (4, 5, 6, 7, 2, 3, 1, 0):
        back(k, 1).start()
    best = jnp.maximum(best, masked_max(scores(keys, rows_own), key_codes == p_own))
    res[0] = best
    for k in SEND_ORDER:
        back(k, 0).start()
    ret[0, d] = best

    for k in range(n_dp):
        back(k, 1).wait_recv()
        if k:
            back(k, 0).wait_recv()
    got = jnp.concatenate([jnp.maximum(ret[0, t], ret[1, t]) for t in range(n_dp)], axis=0)
    picked = lax.dot_general(
        got, lane_hot, (((1,), (0,)), ((), ())),
        preferred_element_type=jnp.float32, precision=lax.Precision.HIGHEST,
    )
    out[...] = jnp.maximum(jnp.sum(t_hot * picked, axis=0, keepdims=True), -1.0)

    for k in (0,) + NEAR + CROSS:
        if k:
            code_copy(k).wait_send()
            back(k, 0).wait_send()
        if k in NEAR:
            block_copy(k).wait_send()
        if k not in CROSS:
            forward(k, 1).wait_send()
        back(k, 1).wait_send()
        forward(k, 0).wait_send()
    for k, h in PIECES:
        block_copy(k, h).wait_send()
        forward(k, 1, h).wait_send()
    codes_copy(0).wait_send()
    codes_copy(1).wait_send()


def fused(embeddings, assignment, pair_list, capacity, n_dp, n_owner):
    rows, width = embeddings.shape
    slots = capacity * n_dp
    block = pltpu.VMEM((n_dp, capacity, width), jnp.bfloat16)
    line = pltpu.VMEM((n_dp, 1, slots), jnp.float32)
    dma = pltpu.SemaphoreType.DMA
    operands = [
        pltpu.with_memory_space_constraint(x, pltpu.HBM)
        for x in (embeddings, assignment.reshape(1, rows), pair_list)
    ]
    best = pl.pallas_call(
        functools.partial(kernel, capacity, n_dp, n_owner),
        out_shape=jax.ShapeDtypeStruct((1, rows), jnp.float32),
        in_specs=[pl.BlockSpec(memory_space=pl.ANY)] * 3,
        out_specs=pl.BlockSpec(memory_space=pltpu.VMEM),
        scratch_shapes=[
            pltpu.VMEM((rows, width), jnp.bfloat16),
            pltpu.VMEM((1, rows), jnp.int32),
            pltpu.SMEM(pair_list.shape, jnp.int32),
            block, block, block, block,
            line, line,
            pltpu.VMEM((3, 1, slots), jnp.float32),
            pltpu.VMEM((3, slots, 128), jnp.float32),
            pltpu.VMEM((2, n_dp, 1, slots), jnp.float32),
            pltpu.VMEM((2, 1, slots), jnp.float32),
            dma((3,)),
            dma((n_dp, 2)), dma((n_dp, 2)), dma((n_dp,)), dma((n_dp,)),
            dma((2, n_dp, 2)), dma((2, n_dp, 2)), dma((2,)), dma((2,)),
            dma((2, n_dp)), dma((2, n_dp)),
        ],
        compiler_params=pltpu.CompilerParams(
            collective_id=0, has_side_effects=True, vmem_limit_bytes=32 * 1024 * 1024
        ),
    )(*operands)
    return best.reshape(rows)


def general(embeddings, assignment, pair_list, capacity, n_dp, n_owner):
    rows, width = embeddings.shape
    slots = capacity * n_dp
    values = embeddings.astype(jnp.float32)
    unit = (values * lax.rsqrt(jnp.sum(values * values, axis=1, keepdims=True) + 1e-06)).astype(
        jnp.bfloat16
    )
    target = assignment // (n_owner * CPD)
    onehot = (target[:, None] == jnp.arange(n_dp, dtype=jnp.int32)[None, :]).astype(jnp.int32)
    slot = jnp.sum(jnp.cumsum(onehot, axis=0) * onehot, axis=1) - 1
    position = target * capacity + slot
    here_owner = lax.axis_index("owner")
    here_dp = lax.axis_index("dp")
    first_id = (here_dp * n_owner + here_owner) * CPD
    partners_mine = lax.dynamic_slice_in_dim(pair_list, first_id, CPD)
    start_best = jnp.full((slots,), -1.0, jnp.float32)
    send_rows = jnp.zeros((slots, width), jnp.bfloat16).at[position].set(unit)
    send_ids = jnp.full((slots,), -1, jnp.int32).at[position].set(assignment)
    got_rows, got_ids = (
        lax.all_to_all(
            send_rows.reshape(n_dp, capacity, width), "dp", split_axis=0, concat_axis=0, tiled=True
        ),
        lax.all_to_all(
            send_ids.reshape(n_dp, capacity), "dp", split_axis=0, concat_axis=0, tiled=True
        ),
    )
    mine = got_rows.reshape(slots, width)
    mine_ids = got_ids.reshape(slots)
    local = jnp.clip(mine_ids - first_id, 0, CPD - 1)
    picked = local[:, None] == jnp.arange(CPD, dtype=jnp.int32)[None, :]
    partner = jnp.sum(jnp.where(picked, partners_mine[None, :], 0), axis=1)
    rows_p = lax.all_gather(mine, "owner", axis=0, tiled=True)
    ids_p = lax.all_gather(mine_ids, "owner", axis=0, tiled=True)
    scores = lax.dot_general(mine, rows_p, NT, preferred_element_type=jnp.float32)
    column = jnp.arange(ids_p.shape[0], dtype=jnp.int32)
    itself = here_owner * slots + jnp.arange(slots, dtype=jnp.int32)
    same = (
        (mine_ids[:, None] == ids_p[None, :])
        & (ids_p[None, :] >= 0)
        & (itself[:, None] != column[None, :])
    )
    related = same | (partner[:, None] == ids_p[None, :])
    best = jnp.maximum(start_best, jnp.max(jnp.where(related, scores, -1.0), axis=1))
    returned = lax.all_to_all(
        best.reshape(n_dp, capacity), "dp", split_axis=0, concat_axis=0, tiled=True
    )
    return returned.reshape(slots)[position]


def shards(embeddings, assignment, pair_list):
    n_dp = lax.axis_size("dp")
    n_owner = lax.axis_size("owner")
    capacity = 2 * embeddings.shape[0] // n_dp
    whole_tiles = n_dp == 8 and n_owner == 4 and capacity % 16 == 0
    form = fused if whole_tiles else general
    return form(embeddings, assignment, pair_list, capacity, n_dp, n_owner)


def solution(mesh):
    placed = (P(("dp", "owner"), None), P(("dp", "owner")), P())
    return jax.shard_map(
        shards, mesh=mesh, in_specs=placed, out_specs=P(("dp", "owner")), check_vma=False
    )
```
